512 devices in a mesh: exp: 8 (over x, y_hi), rows: 64 (over z, y_lo, core).
Axes of the slice: x: 4, y: 8 (y_hi: 2, y_lo: 4; y = y_hi * 4 + y_lo), z: 8, core: 2. Of those that a mesh axis runs over, the one named last changes fastest.
Arguments:
- calib: bfloat16 [20480, 5120], P('rows'), may hold values from -16 to 16
- target: bfloat16 [20480, 768], P('rows', 'exp'), may hold values from -6 to 6
- route: int32 [20480], P('rows'), may hold values from 0 to 7
- base: bfloat16 [5120, 768], P('rows', 'exp'), may hold values from -5 to 5
- up_factor: bfloat16 [8, 5120, 64], P('exp'), may hold values from -3 to 3
- down_factor: bfloat16 [8, 64, 768], P('exp'), may hold values from -3 to 3
Outputs:
- new_base: bfloat16 [5120, 768], P('rows', 'exp')
- new_up: bfloat16 [8, 5120, 64], P('exp')
- new_down: bfloat16 [8, 64, 768], P('exp')
The draws below stay inside these ranges and needn't reach their ends.
All inputs are finite; a program needn't handle non-finite values.
Results may differ from the reference program's by a relative error of at most 0.02.
Values may be sent and summed in bfloat16 or wider, within the bound.
A program may use at most 64 MiB of HBM per device.

```python
import math
import jax
import jax.numpy as jnp
import numpy as np

D = 5120
H = 768
R = 64
ITERS = 2
EXPERTS = 8
TOKENS = 20480


def touch_ends(values, key, least, high):
    extent = values.shape
    spot = [jax.random.randint(jax.random.fold_in(key, axis), (), 0, extent[axis]) for axis in range(len(extent))]
    values = values.at[tuple(spot)].set(least)
    longest = extent.index(max(extent))
    spot[longest] = (spot[longest] + 1) % extent[longest]
    return values.at[tuple(spot)].set(high)


def strengthened(drawn, stream_key, source, target, shards_of, factor):
    owner, partner = [(jnp.arange(drawn.shape[axis_at]) // (drawn.shape[axis_at] // shards_of)).reshape([-1 if axis == axis_at else 1 for axis in range(drawn.ndim)]) for axis_at in (source, target)]
    chosen = jax.random.permutation(stream_key, shards_of)[partner]
    strong = (owner == chosen) | (owner == (partner + shards_of // 2) % shards_of)
    return jnp.where(strong, factor * drawn, drawn)


def steps_of(own_key, extent, pieces, low, top_value):
    level, own = 1.0, jax.random.fold_in(own_key, 6)
    for axis_at, blocks in pieces:
        steps = jnp.exp(jax.random.uniform(jax.random.fold_in(own, axis_at), (blocks,), jnp.float32, low / len(pieces), top_value / len(pieces)))
        level = level * jnp.repeat(steps, extent[axis_at] // blocks).reshape([-1 if axis == axis_at else 1 for axis in range(len(extent))])
    return level


def rank_table(number_of, lean):
    weights = [(1 << 20) // math.isqrt(rank ** lean) + 1 for rank in range(1, number_of + 1)]
    deviation = 1 + sum(weights) // (1 << 30)
    return np.cumsum(np.array([max(1, weight // deviation) for weight in weights]))


def ranked(rng, shape, amount, lean):
    table = rank_table(amount, lean)
    ticket = jax.random.randint(jax.random.fold_in(rng, 1), shape, 0, int(table[amount - 1]))
    rank = jnp.searchsorted(jnp.asarray(table, jnp.int32), ticket, side="right")
    return jax.random.permutation(jax.random.fold_in(rng, 2), amount)[rank].astype(jnp.int32)


def scatter_about(rng, dims, width, reach, pieces=(), dtype=jnp.bfloat16):
    level = steps_of(rng, dims, pieces, -0.22, 0.18) if pieces else 1.0
    entries = jax.random.normal(rng, dims, jnp.float32) * width * level
    return jnp.minimum(jnp.maximum(entries, -reach), reach).astype(dtype)


def noise_with(rng, dims, width, reach, split, heavy, held_as=jnp.bfloat16):
    entries = width * jax.random.normal(rng, dims, jnp.float32)
    if split:
        entries = entries * steps_of(rng, dims, split, -0.22, 0.18)
    return jnp.clip(strengthened(entries, jax.random.fold_in(rng, 3), *heavy), -reach, reach).astype(held_as)


def setup_inputs(seed: int = 0) -> dict:
    streams_of = jax.random.split(jax.random.key(seed), 7)
    calib = noise_with(streams_of[0], (TOKENS, D), 1.0, 16.0, ((0, 64),), (0, 1, 64, 4.0))
    target = scatter_about(streams_of[1], (TOKENS, H), 1.0, 6.0, ((0, 64), (1, 8)))
    route = touch_ends(ranked(streams_of[2], (TOKENS,), EXPERTS, 2), jax.random.fold_in(streams_of[2], 3), 0, EXPERTS - 1).astype(jnp.int32)
    base = scatter_about(streams_of[3], (D, H), 1.0, 5.0, ((0, 64), (1, 8)))
    up_factor = scatter_about(streams_of[4], (EXPERTS, D, R), 0.5, 3.0, ((0, 8),))
    down_factor = scatter_about(streams_of[5], (EXPERTS, R, H), 0.5, 3.0, ((0, 8),))
    return dict(calib=calib, target=target, route=route, base=base, up_factor=up_factor, down_factor=down_factor)


step_rate = 0.25

def reference(calib, target, route, base, up_factor, down_factor):
    inv_d = 1.0 / math.sqrt(D)
    inv_r = 1.0 / math.sqrt(R)
    inv_t = 1.0 / math.sqrt(TOKENS)
    new_base = base
    new_up = up_factor
    new_down = down_factor
    target_wide = target.astype(jnp.float32)
    for step in range(ITERS):
        base_part = (jnp.dot(calib, new_base, preferred_element_type=jnp.float32) * inv_d).astype(jnp.bfloat16)
        inner = jnp.zeros((TOKENS, R), jnp.bfloat16)
        for expert in range(EXPERTS):
            picked = (route == expert)[:, None]
            value = (jnp.dot(calib, new_up[expert], preferred_element_type=jnp.float32) * inv_d).astype(jnp.bfloat16)
            inner = jnp.where(picked, value, inner)
        delta = jnp.zeros((TOKENS, H), jnp.bfloat16)
        for expert in range(EXPERTS):
            picked = (route == expert)[:, None]
            value = (jnp.dot(inner, new_down[expert], preferred_element_type=jnp.float32) * inv_r).astype(jnp.bfloat16)
            delta = jnp.where(picked, value, delta)
        resid = (base_part.astype(jnp.float32) + delta.astype(jnp.float32) - target_wide).astype(jnp.bfloat16)
        grad_base = jnp.dot(calib.T, resid, preferred_element_type=jnp.float32) * inv_t
        ups = []
        downs = []
        for expert in range(EXPERTS):
            picked = (route == expert)[:, None]
            back = (jnp.dot(resid, new_down[expert].T, preferred_element_type=jnp.float32) * inv_r).astype(jnp.bfloat16)
            back = jnp.where(picked, back, jnp.zeros_like(back))
            grad_up = jnp.dot(calib.T, back, preferred_element_type=jnp.float32) * inv_t
            inner_mine = jnp.where(picked, inner, jnp.zeros_like(inner))
            grad_down = jnp.dot(inner_mine.T, resid, preferred_element_type=jnp.float32) * inv_t
            ups.append((new_up[expert].astype(jnp.float32) - step_rate * grad_up).astype(jnp.bfloat16))
            downs.append((new_down[expert].astype(jnp.float32) - step_rate * grad_down).astype(jnp.bfloat16))
        new_base = (new_base.astype(jnp.float32) - step_rate * grad_base).astype(jnp.bfloat16)
        new_up = jnp.stack(ups)
        new_down = jnp.stack(downs)
    return (new_base, new_up, new_down)
```

```python
import functools
import math

import jax
import jax.numpy as jnp
from jax import lax
from jax.experimental import pallas as pl
from jax.experimental.pallas import tpu as pltpu
from jax.sharding import PartitionSpec as P

ITERS = 2
STEP_RATE = 0.25

X, YH, Z, YL = 4, 2, 8, 4
RANK = 64
LANES = 128

f32, bf16 = jnp.float32, jnp.bfloat16
MESH = pl.DeviceIdType.MESH


def dot(a, b):
    return jnp.dot(a, b, preferred_element_type=f32)


def dot_t(a, b):
    return lax.dot_general(a, b, (((1,), (1,)), ((), ())), preferred_element_type=f32)


class Sizes:
    def __init__(self, tok, width, hid, exp_hidden):
        self.t = tok
        self.dh = width // 2
        self.hc = hid
        self.zh = Z // 2
        self.cw = width // Z
        self.nt = self.cw // LANES
        self.db = width // (Z * YL * 2)
        self.experts = X * YH
        self.el = self.experts * RANK // 2
        self.lb = self.el // LANES
        self.dr = hid // 2
        self.na_base = self.nt * hid
        self.na = self.na_base + self.dr
        step = 16 * YL
        self.na_pad = -(-self.na // step) * step
        self.nb = self.nt * RANK
        self.pa = self.na_pad // YL
        self.pb = self.nb // YL
        assert self.zh == 2 * self.lb and self.pb % 16 == 0 and self.na % 16 == 0


def scratch_of(s):
    zr, zl = Z // 2, Z // 2 - 1
    vm = pltpu.VMEM
    return dict(
        calh=vm((2 * s.t, s.dh), bf16),
        uph=vm((s.dh, RANK), bf16),
        bpad=vm((s.db, LANES), bf16),
        bg=vm((s.cw, LANES), bf16),
        tpad=vm((s.t, LANES), f32),
        d0s=vm((s.experts, s.hc, LANES), bf16),
        d0r=vm((s.experts, s.hc, LANES), bf16),
        a=vm((ITERS + 1, s.zh, s.na_pad, LANES), bf16),
        b=vm((ITERS + 1, s.zh, s.nb, LANES), bf16),
        bo=vm((s.zh, s.nb, LANES), bf16),
        dn=vm((ITERS, 2, s.hc, s.el), bf16),
        dnr=vm((ITERS, s.zh, s.dr, LANES), bf16),
        ga=vm((s.zh, s.na, LANES), f32),
        gb=vm((s.zh, s.nb, LANES), f32),
        asr=vm((ITERS, zr, s.na, LANES), bf16),
        arr=vm((ITERS, zr, s.na, LANES), bf16),
        asl=vm((ITERS, zl, s.na, LANES), bf16),
        arl=vm((ITERS, zl, s.na, LANES), bf16),
        bsr=vm((ITERS, zr, s.nb, LANES), bf16),
        brr=vm((ITERS, zr, s.nb, LANES), bf16),
        bsl=vm((ITERS, zl, s.nb, LANES), bf16),
        brl=vm((ITERS, zl, s.nb, LANES), bf16),
        ya=vm((YL, s.pa, LANES), f32),
        yas=vm((ITERS, YL, s.pa, LANES), bf16),
        yar=vm((ITERS, YL, s.pa, LANES), bf16),
        yb=vm((YL, s.pb, LANES), f32),
        ybs=vm((ITERS, YL, s.pb, LANES), bf16),
        ybr=vm((ITERS, YL, s.pb, LANES), bf16),
        xin_s=vm((ITERS, s.t // 2, LANES), f32),
        xin_r=vm((ITERS, s.t // 2, LANES), f32),
        xb_s=vm((ITERS, s.t, LANES), f32),
        xb_r=vm((ITERS, s.t, LANES), f32),
        e1s=vm((ITERS, 2, s.t // 2, LANES), bf16),
        e1r=vm((ITERS, 2, s.t // 2, LANES), bf16),
        e2s=vm((ITERS, 2, s.t // 2, LANES), bf16),
        e2r=vm((ITERS, 2, X, s.t // 2, LANES), bf16),
        ixs=vm((ITERS, 2, s.t, s.el), bf16),
        ixc=vm((ITERS, 2, s.t, s.el), bf16),
        res=vm((ITERS, 2, s.t, LANES), bf16),
        back=vm((ITERS, 2, s.t, LANES), bf16),
        bfin=vm((s.na_base, LANES), bf16),
        fin=vm((s.cw, LANES), f32),
        dnf=vm((s.experts, 2, s.dr, LANES), bf16),
        local_sem=pltpu.SemaphoreType.DMA((4,)),
    )


def kernel(s, n_sem, calib, target, route, base, up, down, o_base, o_up, o_down, *, send, recv,
           calh, uph, bpad, bg, tpad, d0s, d0r, a, b, bo, dn, dnr, ga, gb, asr, arr, asl, arl,
           bsr, brr, bsl, brl, ya, yas, yar, yb, ybs, ybr, xin_s, xin_r, xb_s, xb_r,
           e1s, e1r, e2s, e2r, ixs, ixc, res, back, bfin, fin, dnf, local_sem):
    t, zh, zr, zl = s.t, s.zh, Z // 2, Z // 2 - 1
    width = 2 * s.dh
    inv_d = 1.0 / math.sqrt(width)
    inv_r = 1.0 / math.sqrt(RANK)
    inv_t = 1.0 / math.sqrt(t * Z * YL * 2)

    e, r = lax.axis_index("exp"), lax.axis_index("rows")
    x, yh = e // YH, e % YH
    c, y, z = r % 2, (r // 2) % YL, r // (2 * YL)
    cz = z // zh
    zi = z % zh
    mine = cz == c
    other_core = cz != c
    row_of = lambda z_, y_, c_: (z_ * YL + y_) * 2 + c_
    partner = (e, row_of(z, y, 1 - c))
    right = (e, row_of((z + 1) % Z, y, c))
    left = (e, row_of((z + Z - 1) % Z, y, c))

    used = [0]
    sends = []

    def slot(n=1):
        used[0] += n
        assert used[0] <= n_sem
        return used[0] - n

    def rcopy(src, dst, ss, rs, dev):
        return pltpu.make_async_remote_copy(
            src_ref=src, dst_ref=dst, send_sem=send.at[ss], recv_sem=recv.at[rs],
            device_id=dev, device_id_type=MESH)

    def push(src, dst, ss, rs, dev, cond=None, like=None):
        rcopy(src, dst, ss, rs, dev).start()
        sends.append((cond, like or (lambda: src), ss))

    def landed(dst, rs):
        rcopy(dst, dst, rs, rs, partner).wait_recv()

    lane = lax.broadcasted_iota(jnp.int32, (t // 2, LANES), 1) < RANK

    def pack(v):
        return jnp.where(lane, v[: t // 2], v[t // 2 :])

    def unpack(v):
        w = pltpu.roll(v, RANK, 1)
        return jnp.concatenate([jnp.where(lane, v, w), jnp.where(lane, w, v)], axis=0)

    own_rows = pl.ds(pl.multiple_of(c * t, t), t)
    oth_rows = pl.ds(pl.multiple_of((1 - c) * t, t), t)
    own_cols = pl.ds(pl.multiple_of(c * s.dh, LANES), s.dh)
    oth_cols = pl.ds(pl.multiple_of((1 - c) * s.dh, LANES), s.dh)
    own_half = pl.ds(pl.multiple_of(c * s.dh, 16), s.dh)
    ld_cal = pltpu.make_async_copy(calib.at[:, own_cols], calh.at[own_rows], local_sem.at[0])
    ld_up = pltpu.make_async_copy(up.at[own_half], uph, local_sem.at[1])
    ld_cal.start()
    ld_up.start()

    bar = pltpu.get_barrier_semaphore()
    peers = [partner, right, left]
    for dy in range(1, YL):
        for c_ in (c, 1 - c):
            peers.append((e, row_of(z, (y + dy) % YL, c_)))
    for de in range(1, s.experts):
        peers.append(((e + de) % s.experts, r))
    for dev in peers:
        pl.semaphore_signal(bar, inc=1, device_id=dev, device_id_type=MESH)
    bpad[...] = jnp.zeros_like(bpad)
    bpad[:, : s.hc] = base[...]
    pl.semaphore_wait(bar, len(peers))

    gather_s, gather_r = slot(YL), slot(2 * YL)
    bg_rows = lambda y_, c_: pl.ds(pl.multiple_of((2 * y_ + c_) * s.db, 16), s.db)
    for dy in range(1, YL):
        push(bpad, bg.at[bg_rows(y, c)], gather_s + dy, gather_r + 2 * y + c,
             (e, row_of(z, (y + dy) % YL, cz)))

    @pl.when(other_core)
    def _():
        push(bpad, bg.at[bg_rows(y, c)], gather_s, gather_r + 2 * y + c, partner, other_core)

    @pl.when(mine)
    def _():
        bg[bg_rows(y, c), :] = bpad[...]

    cal_i = slot()
    push(calib.at[:, oth_cols], calh.at[own_rows], cal_i, cal_i, partner)

    dt = jnp.concatenate([down[...].astype(f32), jnp.zeros_like(down, dtype=f32)], axis=0).T
    for j in range(s.experts):
        d0s[j] = dt[j * s.hc : (j + 1) * s.hc].astype(bf16)
    d0_s, d0_r = slot(s.experts), slot(s.experts)
    for de in range(1, s.experts):
        other = (e + de) % s.experts
        push(d0s.at[other], d0r.at[e], d0_s + de, d0_r + de, (other, r))
    d0r[e] = d0s[e]
    tpad[...] = jnp.zeros_like(tpad)
    tpad[:, : s.hc] = target[...].astype(f32)
    a[0, :, s.na :, :] = jnp.zeros((zh, s.na_pad - s.na, LANES), bf16)

    ld_up.wait()
    for k in range(zh):
        for i in range(s.nt):
            lo = k * s.cw + i * LANES
            tile = uph[lo : lo + LANES, :].astype(f32)
            tile = jnp.concatenate([tile, tile], axis=1).T
            b[0, k, i * RANK : (i + 1) * RANK, :] = tile[:RANK].astype(bf16)

    def ag_maker(buf, v, lo, n):
        ss_r, rs_r = slot(zr), slot(zr)
        ss_l, rs_l = slot(max(zl, 1)), slot(max(zl, 1))
        view = lambda k: buf.at[v, k % zh, pl.ds(lo, n)]
        like = lambda: buf.at[v, 0, pl.ds(lo, n)]

        def step(i):
            k = (z + Z - i) % Z
            on = k // zh == c

            @pl.when(on)
            def _():
                if i > 0:
                    landed(view(k), rs_r + i - 1)
                if i < zr:
                    push(view(k), view(k), ss_r + i, rs_r + i, right, on, like)

            if i <= zl:
                k2 = (z + i) % Z
                on2 = k2 // zh == c

                @pl.when(on2)
                def _():
                    if i > 0:
                        landed(view(k2), rs_l + i - 1)
                    if i < zl:
                        push(view(k2), view(k2), ss_l + i, rs_l + i, left, on2, like)

        return step

    def rs_maker(it, g, sr, rr, sl, rl):
        ss_r, rs_r = slot(zr), slot(zr)
        ss_l, rs_l = slot(zl), slot(zl)

        def step(i):
            d = (z + zr - i) % Z
            on = d // zh == c

            @pl.when(on)
            def _():
                val = g[d % zh]
                if i > 0:
                    landed(rr.at[it, i - 1], rs_r + i - 1)
                    val = val + rr[it, i - 1].astype(f32)
                sr[it, i] = val.astype(bf16)
                push(sr.at[it, i], rr.at[it, i], ss_r + i, rs_r + i, right, on,
                     lambda: sr.at[it, i])

            if i < zl:
                d2 = (z + Z - zl + i) % Z
                on2 = d2 // zh == c

                @pl.when(on2)
                def _():
                    val = g[d2 % zh]
                    if i > 0:
                        landed(rl.at[it, i - 1], rs_l + i - 1)
                        val = val + rl[it, i - 1].astype(f32)
                    sl[it, i] = val.astype(bf16)
                    push(sl.at[it, i], rl.at[it, i], ss_l + i, rs_l + i, left, on2,
                         lambda: sl.at[it, i])

        def total():
            landed(rr.at[it, zr - 1], rs_r + zr - 1)
            landed(rl.at[it, zl - 1], rs_l + zl - 1)
            return g[zi] + rr[it, zr - 1].astype(f32) + rl[it, zl - 1].astype(f32)

        return step, total

    def y_maker(it, total, buf, full, send_buf, recv_buf, piece):
        s1, r1 = slot(YL), slot(YL)
        s2, r2 = slot(YL), slot(YL)
        rows = lambda y_: pl.ds(pl.multiple_of(y_ * piece, 16), piece)

        def first():
            @pl.when(mine)
            def _():
                val = total()
                gap = YL * piece - val.shape[0]
                if gap:
                    val = jnp.concatenate([val, jnp.zeros((gap, LANES), f32)], axis=0)
                val = val.reshape(YL, piece, LANES)
                full[...] = val
                send_buf[it] = val.astype(bf16)
                for dy in range(1, YL):
                    o = (y + dy) % YL
                    push(send_buf.at[it, o], recv_buf.at[it, y], s1 + dy, r1 + dy,
                         (e, row_of(z, o, c)), mine, lambda: send_buf.at[it, 0])

        def second():
            @pl.when(mine)
            def _():
                val = full[y]
                for dy in range(1, YL):
                    o = (y + YL - dy) % YL
                    landed(recv_buf.at[it, o], r1 + dy)
                    val = val + recv_buf[it, o].astype(f32)
                old = buf[it, zi, rows(y), :].astype(f32)
                buf[it + 1, zi, rows(y), :] = (old - STEP_RATE * val).astype(bf16)
                for dy in range(1, YL):
                    push(buf.at[it + 1, zi, rows(y)], buf.at[it + 1, zi, rows(y)], s2 + dy,
                         r2 + dy, (e, row_of(z, (y + dy) % YL, c)), mine,
                         lambda: buf.at[it + 1, 0, pl.ds(0, piece)])

        def third():
            @pl.when(mine)
            def _():
                for dy in range(1, YL):
                    landed(buf.at[it + 1, zi, rows((y + YL - dy) % YL)], r2 + dy)

        return first, second, third

    def exp_maker(it, w):
        i1, s2, r2 = slot(), slot(X), slot(X)
        peer = (x * YH + 1 - yh, r)

        def first(val):
            e1s[it, w] = val.astype(bf16)
            push(e1s.at[it, w], e1r.at[it, w], i1, i1, peer)

        def second():
            landed(e1r.at[it, w], i1)
            e2s[it, w] = (e1s[it, w].astype(f32) + e1r[it, w].astype(f32)).astype(bf16)
            for dx in range(1, X):
                push(e2s.at[it, w], e2r.at[it, w, dx], s2 + dx, r2 + dx,
                     (((x + dx) % X) * YH + yh, r))

        def third():
            val = e2s[it, w].astype(f32)
            for dx in range(1, X):
                landed(e2r.at[it, w, dx], r2 + dx)
                val = val + e2r[it, w, dx].astype(f32)
            return val

        return first, second, third

    @pl.when(mine)
    def _():
        for y_ in range(YL):
            for c_ in range(2):
                @pl.when(jnp.logical_not(jnp.logical_and(y_ == y, c_ == c)))
                def _():
                    landed(bg.at[bg_rows(y_, c_)], gather_r + 2 * y_ + c_)
        for i in range(s.nt):
            tile = bg[i * LANES : (i + 1) * LANES, :].astype(f32).T
            a[0, zi, i * s.hc : (i + 1) * s.hc, :] = tile[: s.hc].astype(bf16)

    ag_a = ag_maker(a, 0, 0, s.na_base)
    ag_a(0)
    ag_b = None
    ld_cal.wait()
    mask_own = route[...] == e
    pad_rows = LANES - s.hc

    def hot(h):
        grp = lax.broadcasted_iota(jnp.int32, (t, s.el), 1) // RANK + h * (s.experts // 2)
        return route[...] == grp

    for it in range(ITERS):
        in_i = slot()
        upt = jnp.concatenate(
            [b[it, k, i * RANK : (i + 1) * RANK, :] for k in range(zh) for i in range(s.nt)], axis=1)
        upt = jnp.concatenate([upt, upt], axis=0)
        if it == 0:
            part = dot_t(calh[own_rows, :], upt)
            landed(calh.at[oth_rows], cal_i)
            xin_s[it] = pack(dot_t(calh[oth_rows, :], upt))
            push(xin_s.at[it], xin_r.at[it], in_i, in_i, partner)
        else:
            xin_s[it] = pack(dot_t(calh[oth_rows, :], upt))
            push(xin_s.at[it], xin_r.at[it], in_i, in_i, partner)
            part = dot_t(calh[own_rows, :], upt)
        landed(xin_r.at[it], in_i)
        inner = ((part + unpack(xin_r[it])) * inv_d).astype(bf16).astype(f32)
        inner = jnp.where(mask_own, inner, 0.0)
        x1, x2, x3 = exp_maker(it, 0)
        x1(pack(inner))
        if it == 0:
            ag_a(1)
        x2()
        if it == 0:
            for de in range(1, s.experts):
                landed(d0r.at[(e + s.experts - de) % s.experts], d0_r + de)
            for h in range(2):
                for l in range(s.lb):
                    j = (h * s.lb + l) * 2
                    pair = d0r[j].astype(f32) + pltpu.roll(d0r[j + 1].astype(f32), RANK, 1)
                    dn[0, h, :, l * LANES : (l + 1) * LANES] = pair.astype(bf16)
            for p in range(zh):
                l, h = p // 2, p % 2
                a[0, p, s.na_base : s.na, :] = dn[
                    0, c, h * s.dr : (h + 1) * s.dr, l * LANES : (l + 1) * LANES]
            ag_a(2)
        inner = unpack(x3())
        wide = jnp.concatenate([inner] * s.lb, axis=1)
        for h in range(2):
            ixs[it, h] = jnp.where(hot(h), wide, 0.0).astype(bf16)
        ix_i = slot()
        ixc[it, c] = ixs[it, c]
        push(ixs.at[it, 1 - c], ixc.at[it, c], ix_i, ix_i, partner)
        if it == 0:
            for i in range(3, zr + 1):
                ag_a(i)
        else:
            ag_a(zr)
            dn_i = slot()
            push(a.at[it, :, pl.ds(s.na_base, s.dr)], dnr.at[it], dn_i, dn_i, partner)
        bt = jnp.concatenate(
            [a[it, k, i * s.hc : (i + 1) * s.hc, :] for k in range(zh) for i in range(s.nt)], axis=1)
        if pad_rows:
            bt = jnp.concatenate([bt, jnp.zeros((pad_rows, s.dh), bf16)], axis=0)
        xb_i = slot()
        xb_s[it] = dot_t(calh[oth_rows, :], bt)
        push(xb_s.at[it], xb_r.at[it], xb_i, xb_i, partner)
        part = dot_t(calh[own_rows, :], bt)
        if it > 0:
            landed(dnr.at[it], dn_i)
            for p in range(zh):
                l, h = p // 2, p % 2
                at = (slice(h * s.dr, (h + 1) * s.dr), slice(l * LANES, (l + 1) * LANES))
                dn[(it, c) + at] = a[it, p, s.na_base : s.na, :]
                dn[(it, 1 - c) + at] = dnr[it, p]
        dnw = [dn[it, h] for h in range(2)]
        if pad_rows:
            dnw = [jnp.concatenate([w, jnp.zeros((pad_rows, s.el), bf16)], axis=0) for w in dnw]
        delta = dot_t(ixs[it, 0], dnw[0]) + dot_t(ixs[it, 1], dnw[1])
        delta = (delta * inv_r).astype(bf16).astype(f32)
        landed(xb_r.at[it], xb_i)
        cols = ((part + xb_r[it]) * inv_d).astype(bf16).astype(f32)
        resid = (cols + delta - tpad[...]).astype(bf16)
        res[it, c] = resid
        re_i = slot()
        push(res.at[it, c], res.at[it, c], re_i, re_i, partner)

        fold = jnp.zeros((t, LANES), f32)
        for h in range(2):
            share = jnp.where(hot(h), dot(resid, dnw[h]), 0.0)
            for l in range(s.lb):
                fold = fold + share[:, l * LANES : (l + 1) * LANES]
        fold = (fold + pltpu.roll(fold, RANK, 1)) * inv_r
        b1, b2, b3 = exp_maker(it, 1)
        b1(pack(fold))

        landed(res.at[it, 1 - c], re_i)
        rt = jnp.concatenate([res[it, 0], res[it, 1]], axis=0).astype(f32).T[: s.hc].astype(bf16)
        grad = dot(rt, calh[...]) * inv_t
        for k in range(zh):
            for i in range(s.nt):
                lo = k * s.cw + i * LANES
                ga[k, i * s.hc : (i + 1) * s.hc, :] = grad[:, lo : lo + LANES]
        landed(ixc.at[it, 1 - c], ix_i)
        grad = dot(rt, jnp.concatenate([ixc[it, 0], ixc[it, 1]], axis=0)) * inv_t
        for p in range(zh):
            l, h = p // 2, p % 2
            ga[p, s.na_base : s.na, :] = grad[
                h * s.dr : (h + 1) * s.dr, l * LANES : (l + 1) * LANES]
        rs_a, tot_a = rs_maker(it, ga, asr, arr, asl, arl)
        rs_a(0)
        b2()
        rs_a(1)
        bk = unpack(b3()).astype(bf16).astype(f32)
        back[it, c] = jnp.where(mask_own, bk, 0.0).astype(bf16)
        bk_i = slot()
        push(back.at[it, c], back.at[it, c], bk_i, bk_i, partner)
        landed(back.at[it, 1 - c], bk_i)
        bt = jnp.concatenate([back[it, 0], back[it, 1]], axis=0).astype(f32).T[:RANK].astype(bf16)
        grad = dot(bt, calh[...]) * inv_t
        for k in range(zh):
            for i in range(s.nt):
                lo = k * s.cw + i * LANES
                gb[k, i * RANK : (i + 1) * RANK, :] = grad[:, lo : lo + LANES]
        rs_b, tot_b = rs_maker(it, gb, bsr, brr, bsl, brl)
        rs_b(0)
        for i in range(2, zr):
            rs_a(i)
            rs_b(i - 1)
        ya1, ya2, ya3 = y_maker(it, tot_a, a, ya, yas, yar, s.pa)
        yb1, yb2, yb3 = y_maker(it, tot_b, b, yb, ybs, ybr, s.pb)
        ya1()
        rs_b(zr - 1)
        ya2()
        yb1()
        ya3()
        last = it == ITERS - 1
        ag_b = ag_maker(b, it + 1, 0, s.nb)
        ag_a = ag_maker(a, it + 1, s.na_base, s.dr) if last else ag_maker(a, it + 1, 0, s.na)
        if last:
            bf_i = slot()

            @pl.when(mine)
            def _():
                push(a.at[it + 1, zi, pl.ds(0, s.na_base)], bfin, bf_i, bf_i, partner, mine,
                     lambda: bfin)
                bfin[...] = a[it + 1, zi, : s.na_base, :]

        ag_a(0)
        yb2()
        yb3()
        ag_b(0)
        for i in range(1, zr):
            ag_a(i)
            ag_b(i)
        if not last:
            ag_b(zr)
        else:
            ag_a(zr)

    fs, fr, fc = slot(2 * s.lb), slot(s.experts), slot()
    for l in range(s.lb):
        for h in range(YH):
            other = (s.lb * c + l) * YH + h
            away = other != e
            src = a.at[ITERS, pl.ds(2 * l, 2), pl.ds(s.na_base, s.dr)]

            @pl.when(away)
            def _():
                push(src, dnf.at[e], fs + 2 * l + h, fr + e, (other, r), away, lambda: a.at[ITERS, pl.ds(0, 2), pl.ds(s.na_base, s.dr)])

            @pl.when(other == e)
            def _():
                dnf[e] = a[ITERS, 2 * l : 2 * l + 2, s.na_base : s.na, :]

    @pl.when(other_core)
    def _():
        landed(bfin, bf_i)

    for i in range(s.nt):
        tile = bfin[i * s.hc : (i + 1) * s.hc, :].astype(f32)
        if pad_rows:
            tile = jnp.concatenate([tile, jnp.zeros((pad_rows, LANES), f32)], axis=0)
        fin[i * LANES : (i + 1) * LANES, :] = tile.T
    rows = pl.ds(pl.multiple_of((2 * y + c) * s.db, 16), s.db)
    o_base[...] = fin[rows, :][:, : s.hc].astype(bf16)

    owner = x // s.lb == c

    @pl.when(owner)
    def _():
        for j in range(s.experts):
            @pl.when(j != e)
            def _():
                landed(dnf.at[j], fr + j)
        push(dnf, dnf, fc, fc, partner, owner)

    ag_b(zr)
    fb = slot()
    push(b.at[ITERS], bo, fb, fb, partner)

    @pl.when(jnp.logical_not(owner))
    def _():
        landed(dnf, fc)

    for j in range(s.experts):
        blk = dnf[j].reshape(s.hc, LANES).astype(f32)
        blk = jnp.where(yh == 0, blk, pltpu.roll(blk, RANK, 1))
        o_down[j * s.hc : (j + 1) * s.hc, :] = blk[:, :RANK].astype(bf16)
    o_up[pl.ds(c * zh, zh)] = b[ITERS]
    landed(bo, fb)
    o_up[pl.ds((1 - c) * zh, zh)] = bo[...]

    for cond, src, ss in sends:
        src = src()
        cp = rcopy(src, src, ss, ss, partner)
        if cond is None:
            cp.wait_send()
        else:
            pl.when(cond)(cp.wait_send)


def body(calib, target, route, base, up_factor, down_factor):
    t, width = calib.shape
    s = Sizes(t, width, base.shape[1], down_factor.shape[2])
    n_sem = 320
    any_spec = pl.BlockSpec(memory_space=pl.ANY)
    vmem = pl.BlockSpec(memory_space=pltpu.VMEM)
    scratch = scratch_of(s)
    scratch["send"] = pltpu.SemaphoreType.DMA((n_sem,))
    scratch["recv"] = pltpu.SemaphoreType.DMA((n_sem,))
    hid = down_factor.shape[2]
    o_base, o_up, o_down = pl.pallas_call(
        functools.partial(kernel, s, n_sem),
        out_shape=(
            jax.ShapeDtypeStruct(base.shape, bf16),
            jax.ShapeDtypeStruct((Z, s.nb, LANES), bf16),
            jax.ShapeDtypeStruct((hid, RANK), bf16),
        ),
        in_specs=[any_spec, vmem, vmem, vmem, any_spec, vmem],
        out_specs=(vmem, vmem, vmem),
        scratch_shapes=scratch,
        compiler_params=pltpu.CompilerParams(
            collective_id=0, has_side_effects=True, vmem_limit_bytes=56 * 1024 * 1024
        ),
        name="refine",
    )(calib, target, route[:, None], base, up_factor[0], down_factor[0])
    new_up = o_up.reshape(Z, s.nt, RANK, LANES).transpose(0, 1, 3, 2).reshape(1, width, RANK)
    return o_base, new_up, o_down.T[None]


def solution(mesh):
    in_specs = (
        P("rows", None),
        P("rows", "exp"),
        P("rows"),
        P("rows", "exp"),
        P("exp", None, None),
        P("exp", None, None),
    )
    out_specs = (P("rows", "exp"), P("exp", None, None), P("exp", None, None))
    return jax.shard_map(body, mesh=mesh, in_specs=in_specs, out_specs=out_specs, check_vma=False)
```

```python
import functools
import math

import jax
import jax.numpy as jnp
from jax import lax
from jax.experimental import pallas as pl
from jax.experimental.pallas import tpu as pltpu
from jax.sharding import PartitionSpec as P

ITERS = 2
STEP_RATE = 0.25

X, YH, Z, YL = 4, 2, 8, 4
RANK = 64
LANES = 128

f32, bf16 = jnp.float32, jnp.bfloat16
MESH = pl.DeviceIdType.MESH


def dot(a, b):
    return jnp.dot(a, b, preferred_element_type=f32)


def dot_t(a, b):
    return lax.dot_general(a, b, (((1,), (1,)), ((), ())), preferred_element_type=f32)


class Sizes:
    def __init__(self, tok, width, hid, exp_hidden):
        self.t = tok
        self.dh = width // 2
        self.hc = hid
        self.zh = Z // 2
        self.cw = width // Z
        self.nt = self.cw // LANES
        self.db = width // (Z * YL * 2)
        self.experts = X * YH
        self.el = self.experts * RANK // 2
        self.lb = self.el // LANES
        self.dr = hid // 2
        self.na_base = self.nt * hid
        self.na = self.na_base + self.dr
        step = 16 * YL
        self.na_pad = -(-self.na // step) * step
        self.pa = self.na_pad // YL
        self.pb = RANK // YL
        self.tp = -(-tok // LANES) * LANES
        assert self.zh == 2 * self.lb and self.pb % 16 == 0 and self.na % 16 == 0


def scratch_of(s):
    zr, zl = Z // 2, Z // 2 - 1
    vm = pltpu.VMEM
    return dict(
        calh=vm((2 * s.t, s.dh), bf16),
        uph=vm((RANK, s.dh), bf16),
        tgt=vm((s.hc, s.t), bf16),
        rou=vm((1, s.t), jnp.int32),
        bas=vm((s.db, s.hc), bf16),
        dwn=vm((RANK, s.experts * s.hc), bf16),
        bpad=vm((s.db, LANES), bf16),
        bg=vm((s.cw, LANES), bf16),
        tpad=vm((LANES, s.tp), f32),
        tcol=vm((s.t, LANES), f32),
        rcol=vm((s.t, LANES), f32),
        d0s=vm((s.experts, s.hc, LANES), bf16),
        d0r=vm((s.experts, s.hc, LANES), bf16),
        a=vm((ITERS + 1, s.zh, s.na_pad, LANES), bf16),
        b=vm((ITERS + 1, s.zh, RANK, s.cw), bf16),
        bo=vm((s.zh, RANK, s.cw), bf16),
        dn=vm((ITERS, 2, s.hc, s.el), bf16),
        dnr=vm((ITERS, s.zh, s.dr, LANES), bf16),
        ga=vm((s.zh, s.na, LANES), f32),
        gb=vm((ITERS, s.zh, RANK, s.cw), bf16),
        gbr=vm((ITERS, Z * YL, s.pb, s.cw), bf16),
        asr=vm((ITERS, zr, s.na, LANES), bf16),
        arr=vm((ITERS, zr, s.na, LANES), bf16),
        asl=vm((ITERS, zl, s.na, LANES), bf16),
        arl=vm((ITERS, zl, s.na, LANES), bf16),
        ya=vm((YL, s.pa, LANES), f32),
        yas=vm((ITERS, YL, s.pa, LANES), bf16),
        yar=vm((ITERS, YL, s.pa, LANES), bf16),
        xin_s=vm((ITERS, s.t // 2, LANES), f32),
        xin_r=vm((ITERS, s.t // 2, LANES), f32),
        xb_s=vm((ITERS, s.t, LANES), f32),
        xb_r=vm((ITERS, s.t, LANES), f32),
        e1s=vm((ITERS, 2, s.t // 2, LANES), bf16),
        e1r=vm((ITERS, 2, s.t // 2, LANES), bf16),
        e2s=vm((ITERS, 2, s.t // 2, LANES), bf16),
        e2r=vm((ITERS, 2, X, s.t // 2, LANES), bf16),
        ixs=vm((ITERS, 2, s.t, s.el), bf16),
        ixc=vm((ITERS, 2, s.t, s.el), bf16),
        res=vm((ITERS, 2, s.t, LANES), bf16),
        back=vm((ITERS, 2, s.t, LANES), bf16),
        bfin=vm((s.na_base, LANES), bf16),
        fin=vm((s.cw, LANES), f32),
        dnf=vm((s.experts, 2, s.dr, LANES), bf16),
        fdn=vm((s.experts * s.hc, LANES), f32),
        local_sem=pltpu.SemaphoreType.DMA((6,)),
    )


def kernel(s, n_sem, calib, target, route, base, up, down, o_base, o_up, o_down, *, send, recv,
           calh, uph, tgt, rou, bas, dwn, bpad, bg, tpad, tcol, rcol, d0s, d0r, a, b, bo, dn, dnr,
           ga, gb, gbr, asr, arr, asl, arl, ya, yas, yar, xin_s, xin_r, xb_s, xb_r,
           e1s, e1r, e2s, e2r, ixs, ixc, res, back, bfin, fin, dnf, fdn, local_sem):
    t, zh, zr, zl = s.t, s.zh, Z // 2, Z // 2 - 1
    width = 2 * s.dh
    inv_d = 1.0 / math.sqrt(width)
    inv_r = 1.0 / math.sqrt(RANK)
    inv_t = 1.0 / math.sqrt(t * Z * YL * 2)

    e, r = lax.axis_index("exp"), lax.axis_index("rows")
    x, yh = e // YH, e % YH
    c, y, z = r % 2, (r // 2) % YL, r // (2 * YL)
    cz = z // zh
    zi = z % zh
    mine = cz == c
    other_core = cz != c
    row_of = lambda z_, y_, c_: (z_ * YL + y_) * 2 + c_
    partner = (e, row_of(z, y, 1 - c))
    right = (e, row_of((z + 1) % Z, y, c))
    left = (e, row_of((z + Z - 1) % Z, y, c))

    used = [0]
    sends = []

    def slot(n=1):
        used[0] += n
        assert used[0] <= n_sem
        return used[0] - n

    def rcopy(src, dst, ss, rs, dev):
        return pltpu.make_async_remote_copy(
            src_ref=src, dst_ref=dst, send_sem=send.at[ss], recv_sem=recv.at[rs],
            device_id=dev, device_id_type=MESH)

    def push(src, dst, ss, rs, dev, cond=None, like=None):
        rcopy(src, dst, ss, rs, dev).start()
        sends.append((cond, like or (lambda: src), ss))

    def landed(dst, rs):
        rcopy(dst, dst, rs, rs, partner).wait_recv()

    lane = lax.broadcasted_iota(jnp.int32, (t // 2, LANES), 1) < RANK

    def pack(v):
        return jnp.where(lane, v[: t // 2], v[t // 2 :])

    def unpack(v):
        w = pltpu.roll(v, RANK, 1)
        return jnp.concatenate([jnp.where(lane, v, w), jnp.where(lane, w, v)], axis=0)

    own_rows = pl.ds(pl.multiple_of(c * t, t), t)
    oth_rows = pl.ds(pl.multiple_of((1 - c) * t, t), t)
    own_cols = pl.ds(pl.multiple_of(c * s.dh, LANES), s.dh)
    oth_cols = pl.ds(pl.multiple_of((1 - c) * s.dh, LANES), s.dh)
    ld_cal, ld_up, ld_tgt, ld_rou, ld_bas, ld_dwn = [
        pltpu.make_async_copy(src, dst, local_sem.at[i]) for i, (src, dst) in enumerate((
            (calib.at[:, own_cols], calh.at[own_rows]), (up.at[:, own_cols], uph), (target, tgt),
            (route, rou), (base, bas), (down, dwn)))]
    for ld in (ld_bas, ld_dwn, ld_cal, ld_up, ld_tgt, ld_rou):
        ld.start()

    bar = pltpu.get_barrier_semaphore()
    peers = [partner]
    for dz in range(1, Z):
        peers.append((e, row_of((z + dz) % Z, y, c)))
    for dy in range(1, YL):
        for c_ in (c, 1 - c):
            peers.append((e, row_of(z, (y + dy) % YL, c_)))
    for de in range(1, s.experts):
        peers.append(((e + de) % s.experts, r))
    for dev in peers:
        pl.semaphore_signal(bar, inc=1, device_id=dev, device_id_type=MESH)
    bpad[...] = jnp.zeros_like(bpad)
    ld_bas.wait()
    bpad[:, : s.hc] = bas[...]
    ld_dwn.wait()
    dt = jnp.concatenate([dwn[...].astype(f32), jnp.zeros_like(dwn, dtype=f32)], axis=0).T
    for j in range(s.experts):
        d0s[j] = dt[j * s.hc : (j + 1) * s.hc].astype(bf16)
    pl.semaphore_wait(bar, len(peers))

    gather_s, gather_r = slot(YL), slot(2 * YL)
    bg_rows = lambda y_, c_: pl.ds(pl.multiple_of((2 * y_ + c_) * s.db, 16), s.db)
    for dy in range(1, YL):
        push(bpad, bg.at[bg_rows(y, c)], gather_s + dy, gather_r + 2 * y + c,
             (e, row_of(z, (y + dy) % YL, cz)))

    @pl.when(other_core)
    def _():
        push(bpad, bg.at[bg_rows(y, c)], gather_s, gather_r + 2 * y + c, partner, other_core)

    @pl.when(mine)
    def _():
        bg[bg_rows(y, c), :] = bpad[...]

    cal_i = slot()
    push(calib.at[:, oth_cols], calh.at[own_rows], cal_i, cal_i, partner)

    d0_s, d0_r = slot(s.experts), slot(s.experts)
    for de in range(1, s.experts):
        other = (e + de) % s.experts
        push(d0s.at[other], d0r.at[e], d0_s + de, d0_r + de, (other, r))
    d0r[e] = d0s[e]
    a[0, :, s.na :, :] = jnp.zeros((zh, s.na_pad - s.na, LANES), bf16)

    ld_up.wait()
    for k in range(zh):
        b[0, k] = uph[:, k * s.cw : (k + 1) * s.cw]
    tpad[...] = jnp.zeros_like(tpad)
    ld_tgt.wait()
    tpad[: s.hc, : s.t] = tgt[...].astype(f32)
    tcol[...] = tpad[...].T[: s.t]
    ld_rou.wait()
    tpad[:, : s.t] = jnp.broadcast_to(rou[...].astype(f32), (LANES, s.t))
    rcol[...] = tpad[...].T[: s.t]

    def ag_maker(buf, v, lo, n):
        ss_r, rs_r = slot(zr), slot(zr)
        ss_l, rs_l = slot(max(zl, 1)), slot(max(zl, 1))
        view = lambda k: buf.at[v, k % zh, pl.ds(lo, n)]
        like = lambda: buf.at[v, 0, pl.ds(lo, n)]

        done = set()

        def step(i):
            if i in done:
                return
            done.add(i)
            k = (z + Z - i) % Z
            on = k // zh == c

            @pl.when(on)
            def _():
                if i > 0:
                    landed(view(k), rs_r + i - 1)
                if i < zr:
                    push(view(k), view(k), ss_r + i, rs_r + i, right, on, like)

            if i <= zl:
                k2 = (z + i) % Z
                on2 = k2 // zh == c

                @pl.when(on2)
                def _():
                    if i > 0:
                        landed(view(k2), rs_l + i - 1)
                    if i < zl:
                        push(view(k2), view(k2), ss_l + i, rs_l + i, left, on2, like)

        return step

    def rs_maker(it, g, sr, rr, sl, rl):
        ss_r, rs_r = slot(zr), slot(zr)
        ss_l, rs_l = slot(zl), slot(zl)

        def step(i):
            d = (z + zr - i) % Z
            on = d // zh == c

            @pl.when(on)
            def _():
                val = g[d % zh]
                if i > 0:
                    landed(rr.at[it, i - 1], rs_r + i - 1)
                    val = val + rr[it, i - 1].astype(f32)
                sr[it, i] = val.astype(bf16)
                push(sr.at[it, i], rr.at[it, i], ss_r + i, rs_r + i, right, on,
                     lambda: sr.at[it, i])

            if i < zl:
                d2 = (z + Z - zl + i) % Z
                on2 = d2 // zh == c

                @pl.when(on2)
                def _():
                    val = g[d2 % zh]
                    if i > 0:
                        landed(rl.at[it, i - 1], rs_l + i - 1)
                        val = val + rl[it, i - 1].astype(f32)
                    sl[it, i] = val.astype(bf16)
                    push(sl.at[it, i], rl.at[it, i], ss_l + i, rs_l + i, left, on2,
                         lambda: sl.at[it, i])

        def total():
            landed(rr.at[it, zr - 1], rs_r + zr - 1)
            landed(rl.at[it, zl - 1], rs_l + zl - 1)
            return g[zi] + rr[it, zr - 1].astype(f32) + rl[it, zl - 1].astype(f32)

        return step, total

    def y_maker(it, total, buf, full, send_buf, recv_buf, piece):
        s1, r1 = slot(YL), slot(YL)
        s2, r2 = slot(YL), slot(YL)
        rows = lambda y_: pl.ds(pl.multiple_of(y_ * piece, 16), piece)

        def first():
            @pl.when(mine)
            def _():
                val = total()
                gap = YL * piece - val.shape[0]
                if gap:
                    val = jnp.concatenate([val, jnp.zeros((gap, LANES), f32)], axis=0)
                val = val.reshape(YL, piece, LANES)
                full[...] = val
                send_buf[it] = val.astype(bf16)
                for dy in range(1, YL):
                    o = (y + dy) % YL
                    push(send_buf.at[it, o], recv_buf.at[it, y], s1 + dy, r1 + dy,
                         (e, row_of(z, o, c)), mine, lambda: send_buf.at[it, 0])

        def second():
            @pl.when(mine)
            def _():
                val = full[y]
                for dy in range(1, YL):
                    o = (y + YL - dy) % YL
                    landed(recv_buf.at[it, o], r1 + dy)
                    val = val + recv_buf[it, o].astype(f32)
                old = buf[it, zi, rows(y), :].astype(f32)
                buf[it + 1, zi, rows(y), :] = (old - STEP_RATE * val).astype(bf16)
                for dy in range(1, YL):
                    push(buf.at[it + 1, zi, rows(y)], buf.at[it + 1, zi, rows(y)], s2 + dy,
                         r2 + dy, (e, row_of(z, (y + dy) % YL, c)), mine,
                         lambda: buf.at[it + 1, 0, pl.ds(0, piece)])

        def third():
            @pl.when(mine)
            def _():
                for dy in range(1, YL):
                    landed(buf.at[it + 1, zi, rows((y + YL - dy) % YL)], r2 + dy)

        return first, second, third

    far = sorted(range(Z), key=lambda dz: -min(dz, Z - dz))
    others = [(dz, dy) for dz in far for dy in range(YL) if dz or dy]
    brow = lambda y_: pl.ds(pl.multiple_of(y_ * s.pb, 16), s.pb)
    half_pieces = zh * YL

    def b_maker(it):
        s1, r1, s2, r2 = slot(), slot(), slot(), slot()

        def all_but_own(buf, cnt):
            return lambda: buf.at[it, pl.ds(1, cnt)]

        def first():
            for dz, dy in others:
                z_, y_ = (z + dz) % Z, (y + dy) % YL

                @pl.when(z_ // zh == c)
                def _():
                    place = (Z - dz) % Z * YL + (YL - dy) % YL
                    rcopy(gb.at[it, z_ % zh, brow(y_)], gbr.at[it, place], s1, r1,
                          (e, row_of(z_, y_, c))).start()

            sends.append((mine, all_but_own(gbr, half_pieces - 1), s1))
            sends.append((other_core, all_but_own(gbr, half_pieces), s1))

        def second():
            @pl.when(mine)
            def _():
                landed(gbr.at[it, pl.ds(1, Z * YL - 1)], r1)
                val = gb[it, zi, brow(y), :].astype(f32)
                for i in range(1, Z * YL):
                    val = val + gbr[it, i].astype(f32)
                old = b[it, zi, brow(y), :].astype(f32)
                b[it + 1, zi, brow(y), :] = (old - STEP_RATE * val).astype(bf16)
                for dz, dy in others:
                    piece = b.at[it + 1, zi, brow(y)]
                    rcopy(piece, piece, s2, r2,
                          (e, row_of((z + dz) % Z, (y + dy) % YL, c))).start()

            sends.append((mine, all_but_own(gbr, Z * YL - 1), s2))

        def third():
            @pl.when(mine)
            def _():
                landed(gbr.at[it, pl.ds(1, half_pieces - 1)], r2)

            @pl.when(other_core)
            def _():
                landed(gbr.at[it, pl.ds(1, half_pieces)], r2)

        return first, second, third

    def exp_maker(it, w):
        i1, s2, r2 = slot(), slot(X), slot(X)
        peer = (x * YH + 1 - yh, r)

        def first(val):
            e1s[it, w] = val.astype(bf16)
            push(e1s.at[it, w], e1r.at[it, w], i1, i1, peer)

        def second():
            landed(e1r.at[it, w], i1)
            e2s[it, w] = (e1s[it, w].astype(f32) + e1r[it, w].astype(f32)).astype(bf16)
            for dx in range(1, X):
                push(e2s.at[it, w], e2r.at[it, w, dx], s2 + dx, r2 + dx,
                     (((x + dx) % X) * YH + yh, r))

        def third():
            val = e2s[it, w].astype(f32)
            for dx in range(1, X):
                landed(e2r.at[it, w, dx], r2 + dx)
                val = val + e2r[it, w, dx].astype(f32)
            return val

        return first, second, third

    @pl.when(mine)
    def _():
        for y_ in range(YL):
            for c_ in range(2):
                @pl.when(jnp.logical_not(jnp.logical_and(y_ == y, c_ == c)))
                def _():
                    landed(bg.at[bg_rows(y_, c_)], gather_r + 2 * y_ + c_)
        for i in range(s.nt):
            tile = bg[i * LANES : (i + 1) * LANES, :].astype(f32).T
            a[0, zi, i * s.hc : (i + 1) * s.hc, :] = tile[: s.hc].astype(bf16)

    a0_s, a0_r = slot(Z), slot(zh)
    base_of = lambda k: a.at[0, k, pl.ds(0, s.na_base)]
    for dz in far[:-1]:
        @pl.when(mine)
        def _():
            push(base_of(zi), base_of(zi), a0_s + dz, a0_r + zi, (e, row_of((z + dz) % Z, y, c)),
                 mine, lambda: base_of(0))

    ld_cal.wait()
    mask_own = rcol[...] == e.astype(f32)
    pad_rows = LANES - s.hc

    def hot(h):
        grp = lax.broadcasted_iota(jnp.int32, (t, s.el), 1) // RANK + h * (s.experts // 2)
        return jnp.concatenate([rcol[...]] * s.lb, axis=1) == grp.astype(f32)

    for it in range(ITERS):
        in_i = slot()
        upt = jnp.concatenate([b[it, k] for k in range(zh)], axis=1)
        upt = jnp.concatenate([upt, upt], axis=0)
        if it == 0:
            part = dot_t(calh[own_rows, :], upt)
            landed(calh.at[oth_rows], cal_i)
            xin_s[it] = pack(dot_t(calh[oth_rows, :], upt))
            push(xin_s.at[it], xin_r.at[it], in_i, in_i, partner)
        else:
            xin_s[it] = pack(dot_t(calh[oth_rows, :], upt))
            push(xin_s.at[it], xin_r.at[it], in_i, in_i, partner)
            part = dot_t(calh[own_rows, :], upt)
        landed(xin_r.at[it], in_i)
        inner = ((part + unpack(xin_r[it])) * inv_d).astype(bf16).astype(f32)
        inner = jnp.where(mask_own, inner, 0.0)
        x1, x2, x3 = exp_maker(it, 0)
        x1(pack(inner))
        if it > 0:
            ag_a(zr - 2)
        x2()
        if it == 0:
            for de in range(1, s.experts):
                landed(d0r.at[(e + s.experts - de) % s.experts], d0_r + de)
            for h in range(2):
                for l in range(s.lb):
                    j = (h * s.lb + l) * 2
                    pair = d0r[j].astype(f32) + pltpu.roll(d0r[j + 1].astype(f32), RANK, 1)
                    dn[0, h, :, l * LANES : (l + 1) * LANES] = pair.astype(bf16)
            for p in range(zh):
                l, h = p // 2, p % 2
                a[0, p, s.na_base : s.na, :] = dn[
                    0, c, h * s.dr : (h + 1) * s.dr, l * LANES : (l + 1) * LANES]
        else:
            ag_a(zr - 1)
        inner = unpack(x3())
        wide = jnp.concatenate([inner] * s.lb, axis=1)
        for h in range(2):
            ixs[it, h] = jnp.where(hot(h), wide, 0.0).astype(bf16)
        ix_i = slot()
        ixc[it, c] = ixs[it, c]
        push(ixs.at[it, 1 - c], ixc.at[it, c], ix_i, ix_i, partner)
        if it == 0:
            for k in range(zh):
                @pl.when(c * zh + k != z)
                def _():
                    landed(base_of(k), a0_r + k)
        else:
            ag_a(zr)
            dn_i = slot()
            push(a.at[it, :, pl.ds(s.na_base, s.dr)], dnr.at[it], dn_i, dn_i, partner)
        bt = jnp.concatenate(
            [a[it, k, i * s.hc : (i + 1) * s.hc, :] for k in range(zh) for i in range(s.nt)], axis=1)
        if pad_rows:
            bt = jnp.concatenate([bt, jnp.zeros((pad_rows, s.dh), bf16)], axis=0)
        xb_i = slot()
        xb_s[it] = dot_t(calh[oth_rows, :], bt)
        push(xb_s.at[it], xb_r.at[it], xb_i, xb_i, partner)
        part = dot_t(calh[own_rows, :], bt)
        if it > 0:
            landed(dnr.at[it], dn_i)
            for p in range(zh):
                l, h = p // 2, p % 2
                at = (slice(h * s.dr, (h + 1) * s.dr), slice(l * LANES, (l + 1) * LANES))
                dn[(it, c) + at] = a[it, p, s.na_base : s.na, :]
                dn[(it, 1 - c) + at] = dnr[it, p]
        dnw = [dn[it, h] for h in range(2)]
        if pad_rows:
            dnw = [jnp.concatenate([w, jnp.zeros((pad_rows, s.el), bf16)], axis=0) for w in dnw]
        delta = dot_t(ixs[it, 0], dnw[0]) + dot_t(ixs[it, 1], dnw[1])
        delta = (delta * inv_r).astype(bf16).astype(f32)
        landed(xb_r.at[it], xb_i)
        cols = ((part + xb_r[it]) * inv_d).astype(bf16).astype(f32)
        resid = (cols + delta - tcol[...]).astype(bf16)
        res[it, c] = resid
        re_i = slot()
        push(res.at[it, c], res.at[it, c], re_i, re_i, partner)

        fold = jnp.zeros((t, LANES), f32)
        for h in range(2):
            share = jnp.where(hot(h), dot(resid, dnw[h]), 0.0)
            for l in range(s.lb):
                fold = fold + share[:, l * LANES : (l + 1) * LANES]
        fold = (fold + pltpu.roll(fold, RANK, 1)) * inv_r
        b1, b2, b3 = exp_maker(it, 1)
        b1(pack(fold))

        landed(res.at[it, 1 - c], re_i)
        rt = jnp.concatenate([res[it, 0], res[it, 1]], axis=0).astype(f32).T[: s.hc].astype(bf16)
        grad = dot(rt, calh[...]) * inv_t
        for k in range(zh):
            for i in range(s.nt):
                lo = k * s.cw + i * LANES
                ga[k, i * s.hc : (i + 1) * s.hc, :] = grad[:, lo : lo + LANES]
        landed(ixc.at[it, 1 - c], ix_i)
        grad = dot(rt, jnp.concatenate([ixc[it, 0], ixc[it, 1]], axis=0)) * inv_t
        for p in range(zh):
            l, h = p // 2, p % 2
            ga[p, s.na_base : s.na, :] = grad[
                h * s.dr : (h + 1) * s.dr, l * LANES : (l + 1) * LANES]
        rs_a, tot_a = rs_maker(it, ga, asr, arr, asl, arl)
        rs_a(0)
        b2()
        rs_a(1)
        bk = unpack(b3()).astype(bf16).astype(f32)
        back[it, c] = jnp.where(mask_own, bk, 0.0).astype(bf16)
        bk_i = slot()
        push(back.at[it, c], back.at[it, c], bk_i, bk_i, partner)
        landed(back.at[it, 1 - c], bk_i)
        bt = jnp.concatenate([back[it, 0], back[it, 1]], axis=0).astype(f32).T[:RANK].astype(bf16)
        grad = dot(bt, calh[...]) * inv_t
        for k in range(zh):
            gb[it, k] = grad[:, k * s.cw : (k + 1) * s.cw].astype(bf16)
        yb1, yb2, yb3 = b_maker(it)
        yb1()
        for i in range(2, zr):
            rs_a(i)
        ya1, ya2, ya3 = y_maker(it, tot_a, a, ya, yas, yar, s.pa)
        ya1()
        yb2()
        ya2()
        ya3()
        last = it == ITERS - 1
        ag_a = ag_maker(a, it + 1, s.na_base, s.dr) if last else ag_maker(a, it + 1, 0, s.na)
        ag_a(0)
        if last:
            bf_i = slot()

            @pl.when(mine)
            def _():
                push(a.at[it + 1, zi, pl.ds(0, s.na_base)], bfin, bf_i, bf_i, partner, mine,
                     lambda: bfin)
                bfin[...] = a[it + 1, zi, : s.na_base, :]

        for i in range(1, zr + 1 if last else max(zr - 2, 1)):
            ag_a(i)
        if not last:
            yb3()

    fs, fr, fc = slot(2 * s.lb), slot(s.experts), slot()
    for l in range(s.lb):
        for h in range(YH):
            other = (s.lb * c + l) * YH + h
            away = other != e
            src = a.at[ITERS, pl.ds(2 * l, 2), pl.ds(s.na_base, s.dr)]

            @pl.when(away)
            def _():
                push(src, dnf.at[e], fs + 2 * l + h, fr + e, (other, r), away, lambda: a.at[ITERS, pl.ds(0, 2), pl.ds(s.na_base, s.dr)])

            @pl.when(other == e)
            def _():
                dnf[e] = a[ITERS, 2 * l : 2 * l + 2, s.na_base : s.na, :]

    @pl.when(other_core)
    def _():
        landed(bfin, bf_i)

    for i in range(s.nt):
        tile = bfin[i * s.hc : (i + 1) * s.hc, :].astype(f32)
        if pad_rows:
            tile = jnp.concatenate([tile, jnp.zeros((pad_rows, LANES), f32)], axis=0)
        fin[i * LANES : (i + 1) * LANES, :] = tile.T
    rows = pl.ds(pl.multiple_of((2 * y + c) * s.db, 16), s.db)
    o_base[...] = fin[rows, :][:, : s.hc].astype(bf16)

    owner = x // s.lb == c

    @pl.when(owner)
    def _():
        for j in range(s.experts):
            @pl.when(j != e)
            def _():
                landed(dnf.at[j], fr + j)
        push(dnf, dnf, fc, fc, partner, owner)

    yb3()
    fb = slot()
    push(b.at[ITERS], bo, fb, fb, partner)

    @pl.when(jnp.logical_not(owner))
    def _():
        landed(dnf, fc)

    for j in range(s.experts):
        blk = dnf[j].reshape(s.hc, LANES).astype(f32)
        blk = jnp.where(yh == 0, blk, pltpu.roll(blk, RANK, 1))
        fdn[j * s.hc : (j + 1) * s.hc, :] = blk
    o_down[...] = fdn[...].T[:RANK].astype(bf16)
    up_cols = lambda c_, k: pl.ds(pl.multiple_of(c_ * s.dh + k * s.cw, LANES), s.cw)
    for k in range(zh):
        o_up[:, up_cols(c, k)] = b[ITERS, k]
    landed(bo, fb)
    for k in range(zh):
        o_up[:, up_cols(1 - c, k)] = bo[k]

    for cond, src, ss in sends:
        src = src()
        cp = rcopy(src, src, ss, ss, partner)
        if cond is None:
            cp.wait_send()
        else:
            pl.when(cond)(cp.wait_send)


def body(calib, target, route, base, up_factor, down_factor):
    t, width = calib.shape
    s = Sizes(t, width, base.shape[1], down_factor.shape[2])
    n_sem = 320
    any_spec = pl.BlockSpec(memory_space=pl.ANY)
    vmem = pl.BlockSpec(memory_space=pltpu.VMEM)
    scratch = scratch_of(s)
    scratch["send"] = pltpu.SemaphoreType.DMA((n_sem,))
    scratch["recv"] = pltpu.SemaphoreType.DMA((n_sem,))
    hid = down_factor.shape[2]
    o_base, o_up, o_down = pl.pallas_call(
        functools.partial(kernel, s, n_sem),
        out_shape=(
            jax.ShapeDtypeStruct(base.shape, bf16),
            jax.ShapeDtypeStruct((RANK, width), bf16),
            jax.ShapeDtypeStruct((RANK, hid), bf16),
        ),
        in_specs=[any_spec] * 6,
        out_specs=(vmem, vmem, vmem),
        scratch_shapes=scratch,
        compiler_params=pltpu.CompilerParams(
            collective_id=0, has_side_effects=True, vmem_limit_bytes=56 * 1024 * 1024
        ),
        name="refine",
    )(calib, target.T, route[None], base, up_factor[0].T, down_factor[0])
    return o_base, o_up.T[None], o_down[None]


def solution(mesh):
    in_specs = (
        P("rows", None),
        P("rows", "exp"),
        P("rows"),
        P("rows", "exp"),
        P("exp", None, None),
        P("exp", None, None),
    )
    out_specs = (P("rows", "exp"), P("exp", None, None), P("exp", None, None))
    return jax.shard_map(body, mesh=mesh, in_specs=in_specs, out_specs=out_specs, check_vma=False)
```

```python
import functools
import math

import jax
import jax.numpy as jnp
from jax import lax
from jax.experimental import pallas as pl
from jax.experimental.pallas import tpu as pltpu
from jax.sharding import PartitionSpec as P

ITERS = 2
STEP_RATE = 0.25

X, YH, Z, YL = 4, 2, 8, 4
RANK = 64
LANES = 128

f32, bf16 = jnp.float32, jnp.bfloat16
MESH = pl.DeviceIdType.MESH


def dot(a, b):
    return jnp.dot(a, b, preferred_element_type=f32)


def dot_t(a, b):
    return lax.dot_general(a, b, (((1,), (1,)), ((), ())), preferred_element_type=f32)


class Sizes:
    def __init__(self, tok, width, hid, exp_hidden):
        self.t = tok
        self.dh = width // 2
        self.hc = hid
        self.zh = Z // 2
        self.cw = width // Z
        self.nt = self.cw // LANES
        self.db = width // (Z * YL * 2)
        self.experts = X * YH
        self.el = self.experts * RANK // 2
        self.lb = self.el // LANES
        self.dr = hid // 2
        self.na_base = self.nt * hid
        self.na = self.na_base + self.dr
        step = 16 * YL
        self.na_pad = -(-self.na // step) * step
        self.pa = self.na_pad // YL
        self.pb = RANK // YL
        self.tp = -(-tok // LANES) * LANES
        assert self.zh == 2 * self.lb and self.pb % 16 == 0 and self.na % 16 == 0


def scratch_of(s):
    zr, zl = Z // 2, Z // 2 - 1
    vm = pltpu.VMEM
    return dict(
        calh=vm((2 * s.t, s.dh), bf16),
        calo=vm((s.t, s.dh), bf16),
        uph=vm((RANK, s.dh), bf16),
        tgt=vm((s.hc, s.t), bf16),
        rou=vm((1, s.t), jnp.int32),
        bas=vm((s.db, s.hc), bf16),
        dwn=vm((RANK, s.experts * s.hc), bf16),
        bpad=vm((s.db, LANES), bf16),
        bg=vm((s.cw, LANES), bf16),
        tpad=vm((LANES, s.tp), f32),
        tcol=vm((s.t, LANES), f32),
        rcol=vm((s.t, LANES), f32),
        d0s=vm((s.experts, s.hc, LANES), bf16),
        d0r=vm((s.experts, s.hc, LANES), bf16),
        a=vm((ITERS + 1, s.zh, s.na_pad, LANES), bf16),
        b=vm((ITERS + 1, s.zh, RANK, s.cw), bf16),
        bo=vm((s.zh, RANK, s.cw), bf16),
        dn=vm((ITERS, 2, s.hc, s.el), bf16),
        dnr=vm((ITERS, s.zh, s.dr, LANES), bf16),
        ga=vm((ITERS, s.zh, s.na_pad, LANES), bf16),
        gar=vm((ITERS, Z * YL, s.pa, LANES), bf16),
        gb=vm((ITERS, s.zh, RANK, s.cw), bf16),
        gbr=vm((ITERS, Z * YL, s.pb, s.cw), bf16),
        xin_s=vm((ITERS, s.t // 2, LANES), f32),
        xin_r=vm((ITERS, s.t // 2, LANES), f32),
        xb_s=vm((ITERS, s.t, LANES), f32),
        xb_r=vm((ITERS, s.t, LANES), f32),
        e1s=vm((ITERS, 2, s.t // 2, LANES), bf16),
        e1r=vm((ITERS, 2, s.t // 2, LANES), bf16),
        e2s=vm((ITERS, 2, s.t // 2, LANES), bf16),
        e2r=vm((ITERS, 2, X, s.t // 2, LANES), bf16),
        ixs=vm((ITERS, 2, s.t, s.el), bf16),
        ixc=vm((ITERS, 2, s.t, s.el), bf16),
        res=vm((ITERS, 2, s.t, LANES), bf16),
        back=vm((ITERS, 2, s.t, LANES), bf16),
        bfin=vm((s.na_base, LANES), bf16),
        fin=vm((s.cw, LANES), f32),
        dnf=vm((s.experts, 2, s.dr, LANES), bf16),
        fdn=vm((s.experts * s.hc, LANES), f32),
        local_sem=pltpu.SemaphoreType.DMA((7,)),
    )


def kernel(s, n_sem, calib, target, route, base, up, down, o_base, o_up, o_down, *, send, recv,
           calh, calo, uph, tgt, rou, bas, dwn, bpad, bg, tpad, tcol, rcol, d0s, d0r, a, b, bo, dn, dnr,
           ga, gar, gb, gbr, xin_s, xin_r, xb_s, xb_r,
           e1s, e1r, e2s, e2r, ixs, ixc, res, back, bfin, fin, dnf, fdn, local_sem):
    t, zh, zr, zl = s.t, s.zh, Z // 2, Z // 2 - 1
    width = 2 * s.dh
    inv_d = 1.0 / math.sqrt(width)
    inv_r = 1.0 / math.sqrt(RANK)
    inv_t = 1.0 / math.sqrt(t * Z * YL * 2)

    e, r = lax.axis_index("exp"), lax.axis_index("rows")
    x, yh = e // YH, e % YH
    c, y, z = r % 2, (r // 2) % YL, r // (2 * YL)
    cz = z // zh
    zi = z % zh
    mine = cz == c
    other_core = cz != c
    row_of = lambda z_, y_, c_: (z_ * YL + y_) * 2 + c_
    partner = (e, row_of(z, y, 1 - c))
    right = (e, row_of((z + 1) % Z, y, c))
    left = (e, row_of((z + Z - 1) % Z, y, c))

    used = [0]
    sends = []

    def slot(n=1):
        used[0] += n
        assert used[0] <= n_sem
        return used[0] - n

    def rcopy(src, dst, ss, rs, dev):
        return pltpu.make_async_remote_copy(
            src_ref=src, dst_ref=dst, send_sem=send.at[ss], recv_sem=recv.at[rs],
            device_id=dev, device_id_type=MESH)

    def push(src, dst, ss, rs, dev, cond=None, like=None):
        rcopy(src, dst, ss, rs, dev).start()
        sends.append((cond, like or (lambda: src), ss))

    def landed(dst, rs):
        rcopy(dst, dst, rs, rs, partner).wait_recv()

    lane = lax.broadcasted_iota(jnp.int32, (t // 2, LANES), 1) < RANK

    def pack(v):
        return jnp.where(lane, v[: t // 2], v[t // 2 :])

    def unpack(v):
        w = pltpu.roll(v, RANK, 1)
        return jnp.concatenate([jnp.where(lane, v, w), jnp.where(lane, w, v)], axis=0)

    own_rows = pl.ds(pl.multiple_of(c * t, t), t)
    oth_rows = pl.ds(pl.multiple_of((1 - c) * t, t), t)
    own_cols = pl.ds(pl.multiple_of(c * s.dh, LANES), s.dh)
    oth_cols = pl.ds(pl.multiple_of((1 - c) * s.dh, LANES), s.dh)
    ld_cal, ld_up, ld_tgt, ld_rou, ld_bas, ld_dwn, ld_oth = [
        pltpu.make_async_copy(src, dst, local_sem.at[i]) for i, (src, dst) in enumerate((
            (calib.at[:, own_cols], calh.at[own_rows]), (up.at[:, own_cols], uph), (target, tgt),
            (route, rou), (base, bas), (down, dwn), (calib.at[:, oth_cols], calo)))]
    for ld in (ld_bas, ld_dwn, ld_oth, ld_cal, ld_up, ld_tgt, ld_rou):
        ld.start()

    bar = pltpu.get_barrier_semaphore()
    peers = [partner]
    for dz in range(1, Z):
        peers.append((e, row_of((z + dz) % Z, y, c)))
    for dy in range(1, YL):
        for c_ in (c, 1 - c):
            peers.append((e, row_of(z, (y + dy) % YL, c_)))
    for de in range(1, s.experts):
        peers.append(((e + de) % s.experts, r))
    for dev in peers:
        pl.semaphore_signal(bar, inc=1, device_id=dev, device_id_type=MESH)
    bpad[...] = jnp.zeros_like(bpad)
    ld_bas.wait()
    bpad[:, : s.hc] = bas[...]
    ld_dwn.wait()
    dt = jnp.concatenate([dwn[...].astype(f32), jnp.zeros_like(dwn, dtype=f32)], axis=0).T
    for j in range(s.experts):
        d0s[j] = dt[j * s.hc : (j + 1) * s.hc].astype(bf16)
    pl.semaphore_wait(bar, len(peers))

    gather_s, gather_r = slot(YL), slot(2 * YL)
    bg_rows = lambda y_, c_: pl.ds(pl.multiple_of((2 * y_ + c_) * s.db, 16), s.db)
    for dy in range(1, YL):
        push(bpad, bg.at[bg_rows(y, c)], gather_s + dy, gather_r + 2 * y + c,
             (e, row_of(z, (y + dy) % YL, cz)))

    @pl.when(other_core)
    def _():
        push(bpad, bg.at[bg_rows(y, c)], gather_s, gather_r + 2 * y + c, partner, other_core)

    @pl.when(mine)
    def _():
        bg[bg_rows(y, c), :] = bpad[...]

    cal_i = slot()
    ld_oth.wait()
    push(calo, calh.at[own_rows], cal_i, cal_i, partner)

    d0_s, d0_r = slot(s.experts), slot(s.experts)
    for de in range(1, s.experts):
        other = (e + de) % s.experts
        push(d0s.at[other], d0r.at[e], d0_s + de, d0_r + de, (other, r))
    d0r[e] = d0s[e]
    a[0, :, s.na :, :] = jnp.zeros((zh, s.na_pad - s.na, LANES), bf16)

    ld_up.wait()
    for k in range(zh):
        b[0, k] = uph[:, k * s.cw : (k + 1) * s.cw]
    tpad[...] = jnp.zeros_like(tpad)
    ld_tgt.wait()
    tpad[: s.hc, : s.t] = tgt[...].astype(f32)
    tcol[...] = tpad[...].T[: s.t]
    ld_rou.wait()
    tpad[:, : s.t] = jnp.broadcast_to(rou[...].astype(f32), (LANES, s.t))
    rcol[...] = tpad[...].T[: s.t]

    def ag_maker(buf, v, lo, n):
        ss_r, rs_r = slot(zr), slot(zr)
        ss_l, rs_l = slot(max(zl, 1)), slot(max(zl, 1))
        view = lambda k: buf.at[v, k % zh, pl.ds(lo, n)]
        like = lambda: buf.at[v, 0, pl.ds(lo, n)]

        done = set()

        def step(i):
            if i in done:
                return
            done.add(i)
            k = (z + Z - i) % Z
            on = k // zh == c

            @pl.when(on)
            def _():
                if i > 0:
                    landed(view(k), rs_r + i - 1)
                if i < zr:
                    push(view(k), view(k), ss_r + i, rs_r + i, right, on, like)

            if i <= zl:
                k2 = (z + i) % Z
                on2 = k2 // zh == c

                @pl.when(on2)
                def _():
                    if i > 0:
                        landed(view(k2), rs_l + i - 1)
                    if i < zl:
                        push(view(k2), view(k2), ss_l + i, rs_l + i, left, on2, like)

        return step

    far = sorted(range(Z), key=lambda dz: -min(dz, Z - dz))
    others = [(dz, dy) for dz in far for dy in range(YL) if dz or dy]
    half_pieces = zh * YL

    def sum_maker(it, buf, g, got, size, everywhere):
        s1, r1, s2, r2 = slot(), slot(), slot(YL), slot(YL)
        rows = lambda y_: pl.ds(pl.multiple_of(y_ * size, 16), size)

        def some(cnt):
            return lambda: got.at[it, pl.ds(1, cnt)]

        def first():
            for dz, dy in others:
                z_, y_ = (z + dz) % Z, (y + dy) % YL

                @pl.when(z_ // zh == c)
                def _():
                    place = (Z - dz) % Z * YL + (YL - dy) % YL
                    rcopy(g.at[it, z_ % zh, rows(y_)], got.at[it, place], s1, r1,
                          (e, row_of(z_, y_, c))).start()

            sends.append((mine, some(half_pieces - 1), s1))
            sends.append((other_core, some(half_pieces), s1))

        def second():
            @pl.when(mine)
            def _():
                landed(got.at[it, pl.ds(1, Z * YL - 1)], r1)
                val = g[it, zi, rows(y), :].astype(f32)
                for i in range(1, Z * YL):
                    val = val + got[it, i].astype(f32)
                old = buf[it, zi, rows(y), :].astype(f32)
                buf[it + 1, zi, rows(y), :] = (old - STEP_RATE * val).astype(bf16)
                piece = buf.at[it + 1, zi, rows(y)]
                if everywhere:
                    for dz, dy in others:
                        rcopy(piece, piece, s2, r2,
                              (e, row_of((z + dz) % Z, (y + dy) % YL, c))).start()
                else:
                    for dy in range(1, YL):
                        rcopy(piece, piece, s2 + dy, r2 + dy,
                              (e, row_of(z, (y + dy) % YL, c))).start()

            if everywhere:
                sends.append((mine, some(Z * YL - 1), s2))
            else:
                for dy in range(1, YL):
                    sends.append((mine, lambda: got.at[it, 0], s2 + dy))

        def third():
            if everywhere:
                @pl.when(mine)
                def _():
                    landed(got.at[it, pl.ds(1, half_pieces - 1)], r2)

                @pl.when(other_core)
                def _():
                    landed(got.at[it, pl.ds(1, half_pieces)], r2)
            else:
                @pl.when(mine)
                def _():
                    for dy in range(1, YL):
                        landed(buf.at[it + 1, zi, rows((y + YL - dy) % YL)], r2 + dy)

        return first, second, third

    def exp_maker(it, w):
        i1, s2, r2 = slot(), slot(X), slot(X)
        peer = (x * YH + 1 - yh, r)

        def first(val):
            e1s[it, w] = val.astype(bf16)
            push(e1s.at[it, w], e1r.at[it, w], i1, i1, peer)

        def second():
            landed(e1r.at[it, w], i1)
            e2s[it, w] = (e1s[it, w].astype(f32) + e1r[it, w].astype(f32)).astype(bf16)
            for dx in range(1, X):
                push(e2s.at[it, w], e2r.at[it, w, dx], s2 + dx, r2 + dx,
                     (((x + dx) % X) * YH + yh, r))

        def third():
            val = e2s[it, w].astype(f32)
            for dx in range(1, X):
                landed(e2r.at[it, w, dx], r2 + dx)
                val = val + e2r[it, w, dx].astype(f32)
            return val

        return first, second, third

    @pl.when(mine)
    def _():
        for y_ in range(YL):
            for c_ in range(2):
                @pl.when(jnp.logical_not(jnp.logical_and(y_ == y, c_ == c)))
                def _():
                    landed(bg.at[bg_rows(y_, c_)], gather_r + 2 * y_ + c_)
        for i in range(s.nt):
            tile = bg[i * LANES : (i + 1) * LANES, :].astype(f32).T
            a[0, zi, i * s.hc : (i + 1) * s.hc, :] = tile[: s.hc].astype(bf16)

    a0_s, a0_r = slot(Z), slot(zh)
    base_of = lambda k: a.at[0, k, pl.ds(0, s.na_base)]
    for dz in far[:-1]:
        @pl.when(mine)
        def _():
            push(base_of(zi), base_of(zi), a0_s + dz, a0_r + zi, (e, row_of((z + dz) % Z, y, c)),
                 mine, lambda: base_of(0))

    ld_cal.wait()
    mask_own = rcol[...] == e.astype(f32)
    pad_rows = LANES - s.hc

    def hot(h):
        grp = lax.broadcasted_iota(jnp.int32, (t, s.el), 1) // RANK + h * (s.experts // 2)
        return jnp.concatenate([rcol[...]] * s.lb, axis=1) == grp.astype(f32)

    for it in range(ITERS):
        in_i = slot()
        upt = jnp.concatenate([b[it, k] for k in range(zh)], axis=1)
        upt = jnp.concatenate([upt, upt], axis=0)
        if it == 0:
            part = dot_t(calh[own_rows, :], upt)
            landed(calh.at[oth_rows], cal_i)
            xin_s[it] = pack(dot_t(calh[oth_rows, :], upt))
            push(xin_s.at[it], xin_r.at[it], in_i, in_i, partner)
        else:
            xin_s[it] = pack(dot_t(calh[oth_rows, :], upt))
            push(xin_s.at[it], xin_r.at[it], in_i, in_i, partner)
            part = dot_t(calh[own_rows, :], upt)
        landed(xin_r.at[it], in_i)
        inner = ((part + unpack(xin_r[it])) * inv_d).astype(bf16).astype(f32)
        inner = jnp.where(mask_own, inner, 0.0)
        x1, x2, x3 = exp_maker(it, 0)
        x1(pack(inner))
        if it > 0:
            ag_a(zr - 2)
        x2()
        if it == 0:
            for de in range(1, s.experts):
                landed(d0r.at[(e + s.experts - de) % s.experts], d0_r + de)
            for h in range(2):
                for l in range(s.lb):
                    j = (h * s.lb + l) * 2
                    pair = d0r[j].astype(f32) + pltpu.roll(d0r[j + 1].astype(f32), RANK, 1)
                    dn[0, h, :, l * LANES : (l + 1) * LANES] = pair.astype(bf16)
            for p in range(zh):
                l, h = p // 2, p % 2
                a[0, p, s.na_base : s.na, :] = dn[
                    0, c, h * s.dr : (h + 1) * s.dr, l * LANES : (l + 1) * LANES]
        else:
            ag_a(zr - 1)
        inner = unpack(x3())
        wide = jnp.concatenate([inner] * s.lb, axis=1)
        for h in range(2):
            ixs[it, h] = jnp.where(hot(h), wide, 0.0).astype(bf16)
        ix_i = slot()
        ixc[it, c] = ixs[it, c]
        push(ixs.at[it, 1 - c], ixc.at[it, c], ix_i, ix_i, partner)
        if it == 0:
            for k in range(zh):
                @pl.when(c * zh + k != z)
                def _():
                    landed(base_of(k), a0_r + k)
        else:
            ag_a(zr)
            dn_i = slot()
            push(a.at[it, :, pl.ds(s.na_base, s.dr)], dnr.at[it], dn_i, dn_i, partner)
        bt = jnp.concatenate(
            [a[it, k, i * s.hc : (i + 1) * s.hc, :] for k in range(zh) for i in range(s.nt)], axis=1)
        if pad_rows:
            bt = jnp.concatenate([bt, jnp.zeros((pad_rows, s.dh), bf16)], axis=0)
        xb_i = slot()
        xb_s[it] = dot_t(calh[oth_rows, :], bt)
        push(xb_s.at[it], xb_r.at[it], xb_i, xb_i, partner)
        part = dot_t(calh[own_rows, :], bt)
        if it > 0:
            landed(dnr.at[it], dn_i)
            for p in range(zh):
                l, h = p // 2, p % 2
                at = (slice(h * s.dr, (h + 1) * s.dr), slice(l * LANES, (l + 1) * LANES))
                dn[(it, c) + at] = a[it, p, s.na_base : s.na, :]
                dn[(it, 1 - c) + at] = dnr[it, p]
        dnw = [dn[it, h] for h in range(2)]
        if pad_rows:
            dnw = [jnp.concatenate([w, jnp.zeros((pad_rows, s.el), bf16)], axis=0) for w in dnw]
        delta = dot_t(ixs[it, 0], dnw[0]) + dot_t(ixs[it, 1], dnw[1])
        delta = (delta * inv_r).astype(bf16).astype(f32)
        landed(xb_r.at[it], xb_i)
        cols = ((part + xb_r[it]) * inv_d).astype(bf16).astype(f32)
        resid = (cols + delta - tcol[...]).astype(bf16)
        res[it, c] = resid
        re_i = slot()
        push(res.at[it, c], res.at[it, c], re_i, re_i, partner)

        fold = jnp.zeros((t, LANES), f32)
        for h in range(2):
            share = jnp.where(hot(h), dot(resid, dnw[h]), 0.0)
            for l in range(s.lb):
                fold = fold + share[:, l * LANES : (l + 1) * LANES]
        fold = (fold + pltpu.roll(fold, RANK, 1)) * inv_r
        b1, b2, b3 = exp_maker(it, 1)
        b1(pack(fold))

        landed(res.at[it, 1 - c], re_i)
        rt = jnp.concatenate([res[it, 0], res[it, 1]], axis=0).astype(f32).T[: s.hc].astype(bf16)
        grad = dot(rt, calh[...]) * inv_t
        for k in range(zh):
            for i in range(s.nt):
                lo = k * s.cw + i * LANES
                ga[it, k, i * s.hc : (i + 1) * s.hc, :] = grad[:, lo : lo + LANES].astype(bf16)
        landed(ixc.at[it, 1 - c], ix_i)
        grad = dot(rt, jnp.concatenate([ixc[it, 0], ixc[it, 1]], axis=0)) * inv_t
        for p in range(zh):
            l, h = p // 2, p % 2
            ga[it, p, s.na_base : s.na, :] = grad[
                h * s.dr : (h + 1) * s.dr, l * LANES : (l + 1) * LANES].astype(bf16)
        ga[it, :, s.na :, :] = jnp.zeros((zh, s.na_pad - s.na, LANES), bf16)
        ya1, ya2, ya3 = sum_maker(it, a, ga, gar, s.pa, False)
        ya1()
        b2()
        bk = unpack(b3()).astype(bf16).astype(f32)
        back[it, c] = jnp.where(mask_own, bk, 0.0).astype(bf16)
        bk_i = slot()
        push(back.at[it, c], back.at[it, c], bk_i, bk_i, partner)
        landed(back.at[it, 1 - c], bk_i)
        bt = jnp.concatenate([back[it, 0], back[it, 1]], axis=0).astype(f32).T[:RANK].astype(bf16)
        grad = dot(bt, calh[...]) * inv_t
        for k in range(zh):
            gb[it, k] = grad[:, k * s.cw : (k + 1) * s.cw].astype(bf16)
        yb1, yb2, yb3 = sum_maker(it, b, gb, gbr, s.pb, True)
        yb1()
        ya2()
        yb2()
        ya3()
        last = it == ITERS - 1
        if not last:
            ag_a = ag_maker(a, it + 1, 0, s.na)
            for i in range(max(zr - 2, 1)):
                ag_a(i)
        else:
            bf_i, dn_s, dn_r = slot(), slot(Z), slot(zh)
            dn_of = lambda k: a.at[ITERS, k, pl.ds(s.na_base, s.dr)]

            @pl.when(mine)
            def _():
                for dz in far[:-1]:
                    push(dn_of(zi), dn_of(zi), dn_s + dz, dn_r + zi,
                         (e, row_of((z + dz) % Z, y, c)), mine, lambda: dn_of(0))
                push(a.at[ITERS, zi, pl.ds(0, s.na_base)], bfin, bf_i, bf_i, partner, mine,
                     lambda: bfin)
                bfin[...] = a[ITERS, zi, : s.na_base, :]

            for k in range(zh):
                @pl.when(c * zh + k != z)
                def _():
                    landed(dn_of(k), dn_r + k)
        if not last:
            yb3()

    fs, fr, fc = slot(2 * s.lb), slot(s.experts), slot()
    for l in range(s.lb):
        for h in range(YH):
            other = (s.lb * c + l) * YH + h
            away = other != e
            src = a.at[ITERS, pl.ds(2 * l, 2), pl.ds(s.na_base, s.dr)]

            @pl.when(away)
            def _():
                push(src, dnf.at[e], fs + 2 * l + h, fr + e, (other, r), away, lambda: a.at[ITERS, pl.ds(0, 2), pl.ds(s.na_base, s.dr)])

            @pl.when(other == e)
            def _():
                dnf[e] = a[ITERS, 2 * l : 2 * l + 2, s.na_base : s.na, :]

    @pl.when(other_core)
    def _():
        landed(bfin, bf_i)

    for i in range(s.nt):
        tile = bfin[i * s.hc : (i + 1) * s.hc, :].astype(f32)
        if pad_rows:
            tile = jnp.concatenate([tile, jnp.zeros((pad_rows, LANES), f32)], axis=0)
        fin[i * LANES : (i + 1) * LANES, :] = tile.T
    rows = pl.ds(pl.multiple_of((2 * y + c) * s.db, 16), s.db)
    o_base[...] = fin[rows, :][:, : s.hc].astype(bf16)

    owner = x // s.lb == c

    @pl.when(owner)
    def _():
        for j in range(s.experts):
            @pl.when(j != e)
            def _():
                landed(dnf.at[j], fr + j)
        push(dnf, dnf, fc, fc, partner, owner)

    yb3()
    fb = slot()
    push(b.at[ITERS], bo, fb, fb, partner)

    @pl.when(jnp.logical_not(owner))
    def _():
        landed(dnf, fc)

    for j in range(s.experts):
        blk = dnf[j].reshape(s.hc, LANES).astype(f32)
        blk = jnp.where(yh == 0, blk, pltpu.roll(blk, RANK, 1))
        fdn[j * s.hc : (j + 1) * s.hc, :] = blk
    o_down[...] = fdn[...].T[:RANK].astype(bf16)
    up_cols = lambda c_, k: pl.ds(pl.multiple_of(c_ * s.dh + k * s.cw, LANES), s.cw)
    for k in range(zh):
        o_up[:, up_cols(c, k)] = b[ITERS, k]
    landed(bo, fb)
    for k in range(zh):
        o_up[:, up_cols(1 - c, k)] = bo[k]

    for cond, src, ss in sends:
        src = src()
        cp = rcopy(src, src, ss, ss, partner)
        if cond is None:
            cp.wait_send()
        else:
            pl.when(cond)(cp.wait_send)


def body(calib, target, route, base, up_factor, down_factor):
    t, width = calib.shape
    s = Sizes(t, width, base.shape[1], down_factor.shape[2])
    n_sem = 320
    any_spec = pl.BlockSpec(memory_space=pl.ANY)
    vmem = pl.BlockSpec(memory_space=pltpu.VMEM)
    scratch = scratch_of(s)
    scratch["send"] = pltpu.SemaphoreType.DMA((n_sem,))
    scratch["recv"] = pltpu.SemaphoreType.DMA((n_sem,))
    hid = down_factor.shape[2]
    o_base, o_up, o_down = pl.pallas_call(
        functools.partial(kernel, s, n_sem),
        out_shape=(
            jax.ShapeDtypeStruct(base.shape, bf16),
            jax.ShapeDtypeStruct((RANK, width), bf16),
            jax.ShapeDtypeStruct((RANK, hid), bf16),
        ),
        in_specs=[any_spec] * 6,
        out_specs=(vmem, vmem, vmem),
        scratch_shapes=scratch,
        compiler_params=pltpu.CompilerParams(
            collective_id=0, has_side_effects=True, vmem_limit_bytes=56 * 1024 * 1024
        ),
        name="refine",
    )(calib, target.T, route[None], base, up_factor[0].T, down_factor[0])
    return o_base, o_up.T[None], o_down[None]


def solution(mesh):
    in_specs = (
        P("rows", None),
        P("rows", "exp"),
        P("rows"),
        P("rows", "exp"),
        P("exp", None, None),
        P("exp", None, None),
    )
    out_specs = (P("rows", "exp"), P("exp", None, None), P("exp", None, None))
    return jax.shard_map(body, mesh=mesh, in_specs=in_specs, out_specs=out_specs, check_vma=False)
```

```python
import functools
import math

import jax
import jax.numpy as jnp
from jax import lax
from jax.experimental import pallas as pl
from jax.experimental.pallas import tpu as pltpu
from jax.sharding import PartitionSpec as P

ITERS = 2
STEP_RATE = 0.25

X, YH, Z, YL = 4, 2, 8, 4
RANK = 64
LANES = 128

f32, bf16 = jnp.float32, jnp.bfloat16
MESH = pl.DeviceIdType.MESH


def dot(a, b):
    return jnp.dot(a, b, preferred_element_type=f32)


def dot_t(a, b):
    return lax.dot_general(a, b, (((1,), (1,)), ((), ())), preferred_element_type=f32)


class Sizes:
    def __init__(self, tok, width, hid, exp_hidden):
        self.t = tok
        self.dh = width // 2
        self.hc = hid
        self.zh = Z // 2
        self.cw = width // Z
        self.nt = self.cw // LANES
        self.db = width // (Z * YL * 2)
        self.experts = X * YH
        self.el = self.experts * RANK // 2
        self.lb = self.el // LANES
        self.dr = hid // 2
        self.na_base = self.nt * hid
        self.na = self.na_base + self.dr
        step = 16 * YL
        self.na_pad = -(-self.na // step) * step
        self.pa = self.na_pad // YL
        self.pb = RANK // YL
        self.tp = -(-tok // LANES) * LANES
        assert self.zh == 2 * self.lb and self.pb % 16 == 0 and self.na % 16 == 0


def scratch_of(s):
    vm = pltpu.VMEM
    return dict(
        calh=vm((2 * s.t, s.dh), bf16),
        calo=vm((s.t, s.dh), bf16),
        uph=vm((RANK, s.dh), bf16),
        tgt=vm((s.hc, s.t), bf16),
        rou=vm((1, s.t), jnp.int32),
        bas=vm((s.db, s.hc), bf16),
        dwn=vm((RANK, s.experts * s.hc), bf16),
        bpad=vm((s.db, LANES), bf16),
        bg=vm((s.cw, LANES), bf16),
        tpad=vm((LANES, s.tp), f32),
        tcol=vm((s.t, LANES), f32),
        rcol=vm((s.t, LANES), f32),
        d0s=vm((s.experts, s.hc, LANES), bf16),
        d0r=vm((s.experts, s.hc, LANES), bf16),
        a=vm((ITERS + 1, s.zh, s.na_pad, LANES), bf16),
        b=vm((ITERS + 1, s.zh, RANK, s.cw), bf16),
        bo=vm((s.zh, RANK, s.cw), bf16),
        dn=vm((ITERS, 2, s.hc, s.el), bf16),
        dnr=vm((ITERS, s.zh, s.dr, LANES), bf16),
        ga=vm((ITERS, s.zh, s.na_pad, LANES), bf16),
        gar=vm((ITERS, Z * YL, s.pa, LANES), bf16),
        gb=vm((ITERS, s.zh, RANK, s.cw), bf16),
        gbr=vm((ITERS, Z * YL, s.pb, s.cw), bf16),
        xin_s=vm((ITERS, s.t // 2, LANES), f32),
        xin_r=vm((ITERS, s.t // 2, LANES), f32),
        xb_s=vm((ITERS, s.t, LANES), f32),
        xb_r=vm((ITERS, s.t, LANES), f32),
        e1s=vm((ITERS, 2, s.t // 2, LANES), bf16),
        e1r=vm((ITERS, 2, s.t // 2, LANES), bf16),
        e2s=vm((ITERS, 2, s.t // 2, LANES), bf16),
        e2r=vm((ITERS, 2, X, s.t // 2, LANES), bf16),
        ixs=vm((ITERS, 2, s.t, s.el), bf16),
        ixc=vm((ITERS, 2, s.t, s.el), bf16),
        res=vm((ITERS, 2, s.t, LANES), bf16),
        back=vm((ITERS, 2, s.t, LANES), bf16),
        bfin=vm((s.na_base, LANES), bf16),
        fin=vm((s.cw, LANES), f32),
        dnf=vm((s.experts, 2, s.dr, LANES), bf16),
        fdn=vm((s.experts * s.hc, LANES), f32),
        local_sem=pltpu.SemaphoreType.DMA((7,)),
    )


def kernel(s, n_sem, calib, target, route, base, up, down, o_base, o_up, o_down, *, send, recv,
           calh, calo, uph, tgt, rou, bas, dwn, bpad, bg, tpad, tcol, rcol, d0s, d0r, a, b, bo, dn, dnr,
           ga, gar, gb, gbr, xin_s, xin_r, xb_s, xb_r,
           e1s, e1r, e2s, e2r, ixs, ixc, res, back, bfin, fin, dnf, fdn, local_sem):
    t, zh = s.t, s.zh
    width = 2 * s.dh
    inv_d = 1.0 / math.sqrt(width)
    inv_r = 1.0 / math.sqrt(RANK)
    inv_t = 1.0 / math.sqrt(t * Z * YL * 2)

    e, r = lax.axis_index("exp"), lax.axis_index("rows")
    x, yh = e // YH, e % YH
    c, y, z = r % 2, (r // 2) % YL, r // (2 * YL)
    cz = z // zh
    zi = z % zh
    mine = cz == c
    other_core = cz != c
    row_of = lambda z_, y_, c_: (z_ * YL + y_) * 2 + c_
    partner = (e, row_of(z, y, 1 - c))

    used = [0]
    sends = []

    def slot(n=1):
        used[0] += n
        assert used[0] <= n_sem
        return used[0] - n

    def rcopy(src, dst, ss, rs, dev):
        return pltpu.make_async_remote_copy(
            src_ref=src, dst_ref=dst, send_sem=send.at[ss], recv_sem=recv.at[rs],
            device_id=dev, device_id_type=MESH)

    def push(src, dst, ss, rs, dev, cond=None, like=None):
        rcopy(src, dst, ss, rs, dev).start()
        sends.append((cond, like or (lambda: src), ss))

    def landed(dst, rs):
        rcopy(dst, dst, rs, rs, partner).wait_recv()

    lane = lax.broadcasted_iota(jnp.int32, (t // 2, LANES), 1) < RANK

    def pack(v):
        return jnp.where(lane, v[: t // 2], v[t // 2 :])

    def unpack(v):
        w = pltpu.roll(v, RANK, 1)
        return jnp.concatenate([jnp.where(lane, v, w), jnp.where(lane, w, v)], axis=0)

    own_rows = pl.ds(pl.multiple_of(c * t, t), t)
    oth_rows = pl.ds(pl.multiple_of((1 - c) * t, t), t)
    own_cols = pl.ds(pl.multiple_of(c * s.dh, LANES), s.dh)
    oth_cols = pl.ds(pl.multiple_of((1 - c) * s.dh, LANES), s.dh)
    ld_cal, ld_up, ld_tgt, ld_rou, ld_bas, ld_dwn, ld_oth = [
        pltpu.make_async_copy(src, dst, local_sem.at[i]) for i, (src, dst) in enumerate((
            (calib.at[:, own_cols], calh.at[own_rows]), (up.at[:, own_cols], uph), (target, tgt),
            (route, rou), (base, bas), (down, dwn), (calib.at[:, oth_cols], calo)))]
    for ld in (ld_bas, ld_dwn, ld_oth, ld_cal, ld_up, ld_tgt, ld_rou):
        ld.start()

    bar = pltpu.get_barrier_semaphore()
    peers = [partner]
    for dz in range(1, Z):
        peers.append((e, row_of((z + dz) % Z, y, c)))
    for dy in range(1, YL):
        for c_ in (c, 1 - c):
            peers.append((e, row_of(z, (y + dy) % YL, c_)))
    for de in range(1, s.experts):
        peers.append(((e + de) % s.experts, r))
    for dev in peers:
        pl.semaphore_signal(bar, inc=1, device_id=dev, device_id_type=MESH)
    bpad[...] = jnp.zeros_like(bpad)
    ld_bas.wait()
    bpad[:, : s.hc] = bas[...]
    ld_dwn.wait()
    dt = jnp.concatenate([dwn[...].astype(f32), jnp.zeros_like(dwn, dtype=f32)], axis=0).T
    for j in range(s.experts):
        d0s[j] = dt[j * s.hc : (j + 1) * s.hc].astype(bf16)
    pl.semaphore_wait(bar, len(peers))

    gather_s, gather_r = slot(YL), slot(2 * YL)
    bg_rows = lambda y_, c_: pl.ds(pl.multiple_of((2 * y_ + c_) * s.db, 16), s.db)
    for dy in range(1, YL):
        push(bpad, bg.at[bg_rows(y, c)], gather_s + dy, gather_r + 2 * y + c,
             (e, row_of(z, (y + dy) % YL, cz)))

    @pl.when(other_core)
    def _():
        push(bpad, bg.at[bg_rows(y, c)], gather_s, gather_r + 2 * y + c, partner, other_core)

    @pl.when(mine)
    def _():
        bg[bg_rows(y, c), :] = bpad[...]

    cal_i = slot()
    ld_oth.wait()
    push(calo, calh.at[own_rows], cal_i, cal_i, partner)

    a[0, :, s.na :, :] = jnp.zeros((zh, s.na_pad - s.na, LANES), bf16)

    ld_up.wait()
    for k in range(zh):
        b[0, k] = uph[:, k * s.cw : (k + 1) * s.cw]
    tpad[...] = jnp.zeros_like(tpad)
    ld_tgt.wait()
    tpad[: s.hc, : s.t] = tgt[...].astype(f32)
    tcol[...] = tpad[...].T[: s.t]
    ld_rou.wait()
    tpad[:, : s.t] = jnp.broadcast_to(rou[...].astype(f32), (LANES, s.t))
    rcol[...] = tpad[...].T[: s.t]

    def ag_maker(buf, v, n):
        near = Z // 4
        ss, ss2 = slot(2 * near), slot(2 * near)
        whole, half_a, half_b = slot(zh), slot(zh), slot(zh)
        cut = n // 32 * 16
        view = lambda k, lo=0, m=n: buf.at[v, k % zh, pl.ds(lo, m)]
        dev = lambda dz: (e, row_of((z + Z + dz) % Z, y, c))

        def first():
            for q in range(near, 0, -1):
                for i, sign in enumerate((1, -1)):
                    push(view(z), view(z), ss + 2 * (q - 1) + i, whole + zi, dev(sign * q), mine,
                         lambda: view(0))

        def second():
            for i, sign in enumerate((1, -1)):
                k = (z + Z - sign * near) % Z
                on = k // zh == c
                for q in range(near, 0, -1):
                    lo, m, rs = (0, n, whole) if q < near else (
                        (0, cut, half_a) if sign > 0 else (cut, n - cut, half_b))

                    @pl.when(on)
                    def _():
                        if q == near:
                            landed(view(k), whole + k % zh)
                        push(view(k, lo, m), view(k, lo, m), ss2 + 2 * (q - 1) + i, rs + k % zh,
                             dev(sign * q), on, lambda lo=lo, m=m: view(0, lo, m))

        def third():
            for dz in range(1, Z):
                if dz in (near, Z - near):
                    continue
                k = (z + Z - dz) % Z

                @pl.when(k // zh == c)
                def _():
                    if dz == Z // 2:
                        landed(view(k, 0, cut), half_a + k % zh)
                        landed(view(k, cut, n - cut), half_b + k % zh)
                    else:
                        landed(view(k), whole + k % zh)

        return first, second, third

    far = sorted(range(Z), key=lambda dz: -min(dz, Z - dz))
    others = [(dz, dy) for dz in far for dy in range(YL) if dz or dy]
    half_pieces = zh * YL

    def sum_maker(it, buf, g, got, size, everywhere):
        s1, r1, s2, r2 = slot(), slot(), slot(YL), slot(YL)
        rows = lambda y_: pl.ds(pl.multiple_of(y_ * size, 16), size)

        def some(cnt):
            return lambda: got.at[it, pl.ds(1, cnt)]

        def first():
            for dz, dy in others:
                z_, y_ = (z + dz) % Z, (y + dy) % YL

                @pl.when(z_ // zh == c)
                def _():
                    place = (Z - dz) % Z * YL + (YL - dy) % YL
                    rcopy(g.at[it, z_ % zh, rows(y_)], got.at[it, place], s1, r1,
                          (e, row_of(z_, y_, c))).start()

            sends.append((mine, some(half_pieces - 1), s1))
            sends.append((other_core, some(half_pieces), s1))

        def second():
            @pl.when(mine)
            def _():
                landed(got.at[it, pl.ds(1, Z * YL - 1)], r1)
                val = g[it, zi, rows(y), :].astype(f32)
                for i in range(1, Z * YL):
                    val = val + got[it, i].astype(f32)
                old = buf[it, zi, rows(y), :].astype(f32)
                buf[it + 1, zi, rows(y), :] = (old - STEP_RATE * val).astype(bf16)
                piece = buf.at[it + 1, zi, rows(y)]
                if everywhere:
                    for dz, dy in others:
                        rcopy(piece, piece, s2, r2,
                              (e, row_of((z + dz) % Z, (y + dy) % YL, c))).start()
                else:
                    for dy in range(1, YL):
                        rcopy(piece, piece, s2 + dy, r2 + dy,
                              (e, row_of(z, (y + dy) % YL, c))).start()

            if everywhere:
                sends.append((mine, some(Z * YL - 1), s2))
            else:
                for dy in range(1, YL):
                    sends.append((mine, lambda: got.at[it, 0], s2 + dy))

        def third():
            if everywhere:
                @pl.when(mine)
                def _():
                    landed(got.at[it, pl.ds(1, half_pieces - 1)], r2)

                @pl.when(other_core)
                def _():
                    landed(got.at[it, pl.ds(1, half_pieces)], r2)
            else:
                @pl.when(mine)
                def _():
                    for dy in range(1, YL):
                        landed(buf.at[it + 1, zi, rows((y + YL - dy) % YL)], r2 + dy)

        return first, second, third

    def exp_maker(it, w):
        i1, s2, r2 = slot(), slot(X), slot(X)
        peer = (x * YH + 1 - yh, r)

        def first(val):
            e1s[it, w] = val.astype(bf16)
            push(e1s.at[it, w], e1r.at[it, w], i1, i1, peer)

        def second():
            landed(e1r.at[it, w], i1)
            e2s[it, w] = (e1s[it, w].astype(f32) + e1r[it, w].astype(f32)).astype(bf16)
            for dx in range(1, X):
                push(e2s.at[it, w], e2r.at[it, w, dx], s2 + dx, r2 + dx,
                     (((x + dx) % X) * YH + yh, r))

        def third():
            val = e2s[it, w].astype(f32)
            for dx in range(1, X):
                landed(e2r.at[it, w, dx], r2 + dx)
                val = val + e2r[it, w, dx].astype(f32)
            return val

        return first, second, third

    @pl.when(mine)
    def _():
        for y_ in range(YL):
            for c_ in range(2):
                @pl.when(jnp.logical_not(jnp.logical_and(y_ == y, c_ == c)))
                def _():
                    landed(bg.at[bg_rows(y_, c_)], gather_r + 2 * y_ + c_)
        for i in range(s.nt):
            tile = bg[i * LANES : (i + 1) * LANES, :].astype(f32).T
            a[0, zi, i * s.hc : (i + 1) * s.hc, :] = tile[: s.hc].astype(bf16)

    ag1, ag2, ag3 = ag_maker(a, 0, s.na_base)
    pl.when(mine)(ag1)
    ld_cal.wait()
    mask_own = rcol[...] == e.astype(f32)
    pad_rows = LANES - s.hc

    def hot(h):
        grp = lax.broadcasted_iota(jnp.int32, (t, s.el), 1) // RANK + h * (s.experts // 2)
        return jnp.concatenate([rcol[...]] * s.lb, axis=1) == grp.astype(f32)

    for it in range(ITERS):
        in_i = slot()
        upt = jnp.concatenate([b[it, k] for k in range(zh)], axis=1)
        upt = jnp.concatenate([upt, upt], axis=0)
        if it == 0:
            part = dot_t(calh[own_rows, :], upt)
            landed(calh.at[oth_rows], cal_i)
            xin_s[it] = pack(dot_t(calh[oth_rows, :], upt))
            push(xin_s.at[it], xin_r.at[it], in_i, in_i, partner)
        else:
            xin_s[it] = pack(dot_t(calh[oth_rows, :], upt))
            push(xin_s.at[it], xin_r.at[it], in_i, in_i, partner)
            part = dot_t(calh[own_rows, :], upt)
        landed(xin_r.at[it], in_i)
        inner = ((part + unpack(xin_r[it])) * inv_d).astype(bf16).astype(f32)
        inner = jnp.where(mask_own, inner, 0.0)
        x1, x2, x3 = exp_maker(it, 0)
        x1(pack(inner))
        if it == 0:
            ag2()
            d0_s, d0_r = slot(s.experts), slot(s.experts)
            for de in range(1, s.experts):
                other = (e + de) % s.experts
                push(d0s.at[other], d0r.at[e], d0_s + de, d0_r + de, (other, r))
            d0r[e] = d0s[e]
        x2()
        ag3()
        if it > 0:
            dn_i = slot()
            push(a.at[it, :, pl.ds(s.na_base, s.dr)], dnr.at[it], dn_i, dn_i, partner)
        bt = jnp.concatenate(
            [a[it, k, i * s.hc : (i + 1) * s.hc, :] for k in range(zh) for i in range(s.nt)], axis=1)
        if pad_rows:
            bt = jnp.concatenate([bt, jnp.zeros((pad_rows, s.dh), bf16)], axis=0)
        xb_i = slot()
        xb_s[it] = dot_t(calh[oth_rows, :], bt)
        push(xb_s.at[it], xb_r.at[it], xb_i, xb_i, partner)
        part = dot_t(calh[own_rows, :], bt)
        inner = unpack(x3())
        wide = jnp.concatenate([inner] * s.lb, axis=1)
        for h in range(2):
            ixs[it, h] = jnp.where(hot(h), wide, 0.0).astype(bf16)
        ix_i = slot()
        ixc[it, c] = ixs[it, c]
        push(ixs.at[it, 1 - c], ixc.at[it, c], ix_i, ix_i, partner)
        if it == 0:
            for de in range(1, s.experts):
                landed(d0r.at[(e + s.experts - de) % s.experts], d0_r + de)
            for h in range(2):
                for l in range(s.lb):
                    j = (h * s.lb + l) * 2
                    pair = d0r[j].astype(f32) + pltpu.roll(d0r[j + 1].astype(f32), RANK, 1)
                    dn[0, h, :, l * LANES : (l + 1) * LANES] = pair.astype(bf16)
            for p in range(zh):
                l, h = p // 2, p % 2
                a[0, p, s.na_base : s.na, :] = dn[
                    0, c, h * s.dr : (h + 1) * s.dr, l * LANES : (l + 1) * LANES]
        else:
            landed(dnr.at[it], dn_i)
            for p in range(zh):
                l, h = p // 2, p % 2
                at = (slice(h * s.dr, (h + 1) * s.dr), slice(l * LANES, (l + 1) * LANES))
                dn[(it, c) + at] = a[it, p, s.na_base : s.na, :]
                dn[(it, 1 - c) + at] = dnr[it, p]
        dnw = [dn[it, h] for h in range(2)]
        if pad_rows:
            dnw = [jnp.concatenate([w, jnp.zeros((pad_rows, s.el), bf16)], axis=0) for w in dnw]
        delta = dot_t(ixs[it, 0], dnw[0]) + dot_t(ixs[it, 1], dnw[1])
        delta = (delta * inv_r).astype(bf16).astype(f32)
        landed(xb_r.at[it], xb_i)
        cols = ((part + xb_r[it]) * inv_d).astype(bf16).astype(f32)
        resid = (cols + delta - tcol[...]).astype(bf16)
        res[it, c] = resid
        re_i = slot()
        push(res.at[it, c], res.at[it, c], re_i, re_i, partner)

        fold = jnp.zeros((t, LANES), f32)
        for h in range(2):
            share = jnp.where(hot(h), dot(resid, dnw[h]), 0.0)
            for l in range(s.lb):
                fold = fold + share[:, l * LANES : (l + 1) * LANES]
        fold = (fold + pltpu.roll(fold, RANK, 1)) * inv_r
        b1, b2, b3 = exp_maker(it, 1)
        b1(pack(fold))

        landed(res.at[it, 1 - c], re_i)
        rt = jnp.concatenate([res[it, 0], res[it, 1]], axis=0).astype(f32).T[: s.hc].astype(bf16)
        grad = dot(rt, calh[...]) * inv_t
        for k in range(zh):
            for i in range(s.nt):
                lo = k * s.cw + i * LANES
                ga[it, k, i * s.hc : (i + 1) * s.hc, :] = grad[:, lo : lo + LANES].astype(bf16)
        landed(ixc.at[it, 1 - c], ix_i)
        grad = dot(rt, jnp.concatenate([ixc[it, 0], ixc[it, 1]], axis=0)) * inv_t
        for p in range(zh):
            l, h = p // 2, p % 2
            ga[it, p, s.na_base : s.na, :] = grad[
                h * s.dr : (h + 1) * s.dr, l * LANES : (l + 1) * LANES].astype(bf16)
        ga[it, :, s.na :, :] = jnp.zeros((zh, s.na_pad - s.na, LANES), bf16)
        ya1, ya2, ya3 = sum_maker(it, a, ga, gar, s.pa, False)
        ya1()
        b2()
        bk = unpack(b3()).astype(bf16).astype(f32)
        back[it, c] = jnp.where(mask_own, bk, 0.0).astype(bf16)
        bk_i = slot()
        push(back.at[it, c], back.at[it, c], bk_i, bk_i, partner)
        landed(back.at[it, 1 - c], bk_i)
        bt = jnp.concatenate([back[it, 0], back[it, 1]], axis=0).astype(f32).T[:RANK].astype(bf16)
        grad = dot(bt, calh[...]) * inv_t
        for k in range(zh):
            gb[it, k] = grad[:, k * s.cw : (k + 1) * s.cw].astype(bf16)
        yb1, yb2, yb3 = sum_maker(it, b, gb, gbr, s.pb, True)
        yb1()
        ya2()
        yb2()
        ya3()
        last = it == ITERS - 1
        if not last:
            ag1, ag2, ag3 = ag_maker(a, it + 1, s.na)
            pl.when(mine)(ag1)
            ag2()
        else:
            bf_i, dn_s, dn_r = slot(), slot(Z), slot(zh)
            dn_of = lambda k: a.at[ITERS, k, pl.ds(s.na_base, s.dr)]

            @pl.when(mine)
            def _():
                for dz in far[:-1]:
                    push(dn_of(zi), dn_of(zi), dn_s + dz, dn_r + zi,
                         (e, row_of((z + dz) % Z, y, c)), mine, lambda: dn_of(0))
                push(a.at[ITERS, zi, pl.ds(0, s.na_base)], bfin, bf_i, bf_i, partner, mine,
                     lambda: bfin)
                bfin[...] = a[ITERS, zi, : s.na_base, :]

            for k in range(zh):
                @pl.when(c * zh + k != z)
                def _():
                    landed(dn_of(k), dn_r + k)
        if not last:
            yb3()

    fs, fr, fc = slot(2 * s.lb), slot(s.experts), slot()
    for l in range(s.lb):
        for h in range(YH):
            other = (s.lb * c + l) * YH + h
            away = other != e
            src = a.at[ITERS, pl.ds(2 * l, 2), pl.ds(s.na_base, s.dr)]

            @pl.when(away)
            def _():
                push(src, dnf.at[e], fs + 2 * l + h, fr + e, (other, r), away, lambda: a.at[ITERS, pl.ds(0, 2), pl.ds(s.na_base, s.dr)])

            @pl.when(other == e)
            def _():
                dnf[e] = a[ITERS, 2 * l : 2 * l + 2, s.na_base : s.na, :]

    @pl.when(other_core)
    def _():
        landed(bfin, bf_i)

    for i in range(s.nt):
        tile = bfin[i * s.hc : (i + 1) * s.hc, :].astype(f32)
        if pad_rows:
            tile = jnp.concatenate([tile, jnp.zeros((pad_rows, LANES), f32)], axis=0)
        fin[i * LANES : (i + 1) * LANES, :] = tile.T
    rows = pl.ds(pl.multiple_of((2 * y + c) * s.db, 16), s.db)
    o_base[...] = fin[rows, :][:, : s.hc].astype(bf16)

    owner = x // s.lb == c

    @pl.when(owner)
    def _():
        for j in range(s.experts):
            @pl.when(j != e)
            def _():
                landed(dnf.at[j], fr + j)
        push(dnf, dnf, fc, fc, partner, owner)

    yb3()
    fb = slot()
    push(b.at[ITERS], bo, fb, fb, partner)

    @pl.when(jnp.logical_not(owner))
    def _():
        landed(dnf, fc)

    for j in range(s.experts):
        blk = dnf[j].reshape(s.hc, LANES).astype(f32)
        blk = jnp.where(yh == 0, blk, pltpu.roll(blk, RANK, 1))
        fdn[j * s.hc : (j + 1) * s.hc, :] = blk
    o_down[...] = fdn[...].T[:RANK].astype(bf16)
    up_cols = lambda c_, k: pl.ds(pl.multiple_of(c_ * s.dh + k * s.cw, LANES), s.cw)
    for k in range(zh):
        o_up[:, up_cols(c, k)] = b[ITERS, k]
    landed(bo, fb)
    for k in range(zh):
        o_up[:, up_cols(1 - c, k)] = bo[k]

    for cond, src, ss in sends:
        src = src()
        cp = rcopy(src, src, ss, ss, partner)
        if cond is None:
            cp.wait_send()
        else:
            pl.when(cond)(cp.wait_send)


def body(calib, target, route, base, up_factor, down_factor):
    t, width = calib.shape
    s = Sizes(t, width, base.shape[1], down_factor.shape[2])
    n_sem = 320
    any_spec = pl.BlockSpec(memory_space=pl.ANY)
    vmem = pl.BlockSpec(memory_space=pltpu.VMEM)
    scratch = scratch_of(s)
    scratch["send"] = pltpu.SemaphoreType.DMA((n_sem,))
    scratch["recv"] = pltpu.SemaphoreType.DMA((n_sem,))
    hid = down_factor.shape[2]
    o_base, o_up, o_down = pl.pallas_call(
        functools.partial(kernel, s, n_sem),
        out_shape=(
            jax.ShapeDtypeStruct(base.shape, bf16),
            jax.ShapeDtypeStruct((RANK, width), bf16),
            jax.ShapeDtypeStruct((RANK, hid), bf16),
        ),
        in_specs=[any_spec] * 6,
        out_specs=(vmem, vmem, vmem),
        scratch_shapes=scratch,
        compiler_params=pltpu.CompilerParams(
            collective_id=0, has_side_effects=True, vmem_limit_bytes=56 * 1024 * 1024
        ),
        name="refine",
    )(calib, target.T, route[None], base, up_factor[0].T, down_factor[0])
    return o_base, o_up.T[None], o_down[None]


def solution(mesh):
    in_specs = (
        P("rows", None),
        P("rows", "exp"),
        P("rows"),
        P("rows", "exp"),
        P("exp", None, None),
        P("exp", None, None),
    )
    out_specs = (P("rows", "exp"), P("exp", None, None), P("exp", None, None))
    return jax.shard_map(body, mesh=mesh, in_specs=in_specs, out_specs=out_specs, check_vma=False)
```

```python
import functools
import math

import jax
import jax.numpy as jnp
from jax import lax
from jax.experimental import pallas as pl
from jax.experimental.pallas import tpu as pltpu
from jax.sharding import PartitionSpec as P

ITERS = 2
STEP_RATE = 0.25

X, YH, Z, YL = 4, 2, 8, 4
RANK = 64
LANES = 128

f32, bf16 = jnp.float32, jnp.bfloat16
MESH = pl.DeviceIdType.MESH


def dot(a, b):
    return jnp.dot(a, b, preferred_element_type=f32)


def dot_t(a, b):
    return lax.dot_general(a, b, (((1,), (1,)), ((), ())), preferred_element_type=f32)


class Sizes:
    def __init__(self, tok, width, hid, exp_hidden):
        self.t = tok
        self.dh = width // 2
        self.hc = hid
        self.zh = Z // 2
        self.cw = width // Z
        self.nt = self.cw // LANES
        self.db = width // (Z * YL * 2)
        self.experts = X * YH
        self.el = self.experts * RANK // 2
        self.lb = self.el // LANES
        self.dr = hid // 2
        self.na_base = self.nt * hid
        self.na = self.na_base + self.dr
        step = 16 * YL
        self.na_pad = -(-self.na // step) * step
        self.pa = self.na_pad // YL
        self.pb = RANK // YL
        self.tp = -(-tok // LANES) * LANES
        assert self.zh == 2 * self.lb and self.pb % 16 == 0 and self.na % 16 == 0


def scratch_of(s):
    vm = pltpu.VMEM
    return dict(
        calh=vm((2 * s.t, s.dh), bf16),
        calo=vm((s.t, s.dh), bf16),
        uph=vm((RANK, s.dh), bf16),
        tgt=vm((s.hc, s.t), bf16),
        rou=vm((1, s.t), jnp.int32),
        bas=vm((s.db, s.hc), bf16),
        dwn=vm((RANK, s.experts * s.hc), bf16),
        bpad=vm((s.db, LANES), bf16),
        bg=vm((s.cw, LANES), bf16),
        tpad=vm((LANES, s.tp), f32),
        tcol=vm((s.t, LANES), f32),
        rcol=vm((s.t, LANES), f32),
        d0s=vm((s.experts, s.hc, LANES), bf16),
        d0r=vm((s.experts, s.hc, LANES), bf16),
        a=vm((ITERS + 1, s.zh, s.na_pad, LANES), bf16),
        b=vm((ITERS + 1, s.zh, RANK, s.cw), bf16),
        bo=vm((s.zh, RANK, s.cw), bf16),
        dn=vm((ITERS, 2, s.hc, s.el), bf16),
        dnr=vm((ITERS, s.zh, s.dr, LANES), bf16),
        ga=vm((ITERS, s.zh, s.na, LANES), bf16),
        rly=vm((ITERS, 2, Z // 4, s.na, LANES), bf16),
        rsum=vm((ITERS, 2, s.na, LANES), bf16),
        gin=vm((ITERS, 2, Z // 4, s.na, LANES), bf16),
        ya=vm((YL, s.pa, LANES), f32),
        yas=vm((ITERS, YL, s.pa, LANES), bf16),
        yar=vm((ITERS, YL, s.pa, LANES), bf16),
        gb=vm((ITERS, s.zh, RANK, s.cw), bf16),
        gbr=vm((ITERS, Z * YL, s.pb, s.cw), bf16),
        xin_s=vm((ITERS, s.t // 2, LANES), f32),
        xin_r=vm((ITERS, s.t // 2, LANES), f32),
        xb_s=vm((ITERS, s.t, LANES), f32),
        xb_r=vm((ITERS, s.t, LANES), f32),
        e1s=vm((ITERS, 2, s.t // 2, LANES), bf16),
        e1r=vm((ITERS, 2, s.t // 2, LANES), bf16),
        e2s=vm((ITERS, 2, s.t // 2, LANES), bf16),
        e2r=vm((ITERS, 2, X, s.t // 2, LANES), bf16),
        ixs=vm((ITERS, 2, s.t, s.el), bf16),
        ixc=vm((ITERS, 2, s.t, s.el), bf16),
        res=vm((ITERS, 2, s.t, LANES), bf16),
        back=vm((ITERS, 2, s.t, LANES), bf16),
        bfin=vm((s.na_base, LANES), bf16),
        fin=vm((s.cw, LANES), f32),
        dnf=vm((s.experts, 2, s.dr, LANES), bf16),
        fdn=vm((s.experts * s.hc, LANES), f32),
        local_sem=pltpu.SemaphoreType.DMA((7,)),
    )


def kernel(s, n_sem, calib, target, route, base, up, down, o_base, o_up, o_down, *, send, recv,
           calh, calo, uph, tgt, rou, bas, dwn, bpad, bg, tpad, tcol, rcol, d0s, d0r, a, b, bo, dn, dnr,
           ga, rly, rsum, gin, ya, yas, yar, gb, gbr, xin_s, xin_r, xb_s, xb_r,
           e1s, e1r, e2s, e2r, ixs, ixc, res, back, bfin, fin, dnf, fdn, local_sem):
    t, zh = s.t, s.zh
    width = 2 * s.dh
    inv_d = 1.0 / math.sqrt(width)
    inv_r = 1.0 / math.sqrt(RANK)
    inv_t = 1.0 / math.sqrt(t * Z * YL * 2)

    e, r = lax.axis_index("exp"), lax.axis_index("rows")
    x, yh = e // YH, e % YH
    c, y, z = r % 2, (r // 2) % YL, r // (2 * YL)
    cz = z // zh
    zi = z % zh
    mine = cz == c
    other_core = cz != c
    row_of = lambda z_, y_, c_: (z_ * YL + y_) * 2 + c_
    partner = (e, row_of(z, y, 1 - c))

    used = [0]
    sends = []

    def slot(n=1):
        used[0] += n
        assert used[0] <= n_sem
        return used[0] - n

    def rcopy(src, dst, ss, rs, dev):
        return pltpu.make_async_remote_copy(
            src_ref=src, dst_ref=dst, send_sem=send.at[ss], recv_sem=recv.at[rs],
            device_id=dev, device_id_type=MESH)

    def push(src, dst, ss, rs, dev, cond=None, like=None):
        rcopy(src, dst, ss, rs, dev).start()
        sends.append((cond, like or (lambda: src), ss))

    def landed(dst, rs):
        rcopy(dst, dst, rs, rs, partner).wait_recv()

    lane = lax.broadcasted_iota(jnp.int32, (t // 2, LANES), 1) < RANK

    def pack(v):
        return jnp.where(lane, v[: t // 2], v[t // 2 :])

    def unpack(v):
        w = pltpu.roll(v, RANK, 1)
        return jnp.concatenate([jnp.where(lane, v, w), jnp.where(lane, w, v)], axis=0)

    own_rows = pl.ds(pl.multiple_of(c * t, t), t)
    oth_rows = pl.ds(pl.multiple_of((1 - c) * t, t), t)
    own_cols = pl.ds(pl.multiple_of(c * s.dh, LANES), s.dh)
    oth_cols = pl.ds(pl.multiple_of((1 - c) * s.dh, LANES), s.dh)
    ld_cal, ld_up, ld_tgt, ld_rou, ld_bas, ld_dwn, ld_oth = [
        pltpu.make_async_copy(src, dst, local_sem.at[i]) for i, (src, dst) in enumerate((
            (calib.at[:, own_cols], calh.at[own_rows]), (up.at[:, own_cols], uph), (target, tgt),
            (route, rou), (base, bas), (down, dwn), (calib.at[:, oth_cols], calo)))]
    for ld in (ld_bas, ld_dwn, ld_oth, ld_cal, ld_up, ld_tgt, ld_rou):
        ld.start()

    bar = pltpu.get_barrier_semaphore()
    peers = [partner]
    for dz in range(1, Z):
        peers.append((e, row_of((z + dz) % Z, y, c)))
    for dy in range(1, YL):
        for c_ in (c, 1 - c):
            peers.append((e, row_of(z, (y + dy) % YL, c_)))
    for de in range(1, s.experts):
        peers.append(((e + de) % s.experts, r))
    for dev in peers:
        pl.semaphore_signal(bar, inc=1, device_id=dev, device_id_type=MESH)
    bpad[...] = jnp.zeros_like(bpad)
    ld_bas.wait()
    bpad[:, : s.hc] = bas[...]
    ld_dwn.wait()
    dt = jnp.concatenate([dwn[...].astype(f32), jnp.zeros_like(dwn, dtype=f32)], axis=0).T
    for j in range(s.experts):
        d0s[j] = dt[j * s.hc : (j + 1) * s.hc].astype(bf16)
    pl.semaphore_wait(bar, len(peers))

    gather_s, gather_r = slot(YL), slot(2 * YL)
    bg_rows = lambda y_, c_: pl.ds(pl.multiple_of((2 * y_ + c_) * s.db, 16), s.db)
    for dy in range(1, YL):
        push(bpad, bg.at[bg_rows(y, c)], gather_s + dy, gather_r + 2 * y + c,
             (e, row_of(z, (y + dy) % YL, cz)))

    @pl.when(other_core)
    def _():
        push(bpad, bg.at[bg_rows(y, c)], gather_s, gather_r + 2 * y + c, partner, other_core)

    @pl.when(mine)
    def _():
        bg[bg_rows(y, c), :] = bpad[...]

    cal_i = slot()
    ld_oth.wait()
    push(calo, calh.at[own_rows], cal_i, cal_i, partner)

    a[0, :, s.na :, :] = jnp.zeros((zh, s.na_pad - s.na, LANES), bf16)

    ld_up.wait()
    for k in range(zh):
        b[0, k] = uph[:, k * s.cw : (k + 1) * s.cw]
    tpad[...] = jnp.zeros_like(tpad)
    ld_tgt.wait()
    tpad[: s.hc, : s.t] = tgt[...].astype(f32)
    tcol[...] = tpad[...].T[: s.t]
    ld_rou.wait()
    tpad[:, : s.t] = jnp.broadcast_to(rou[...].astype(f32), (LANES, s.t))
    rcol[...] = tpad[...].T[: s.t]

    def ag_maker(buf, v, n):
        near = Z // 4
        ss, ss2 = slot(2 * near), slot(2 * near)
        whole, half_a, half_b = slot(zh), slot(zh), slot(zh)
        cut = n // 32 * 16
        view = lambda k, lo=0, m=n: buf.at[v, k % zh, pl.ds(lo, m)]
        dev = lambda dz: (e, row_of((z + Z + dz) % Z, y, c))

        def first():
            for q in range(near, 0, -1):
                for i, sign in enumerate((1, -1)):
                    push(view(z), view(z), ss + 2 * (q - 1) + i, whole + zi, dev(sign * q), mine,
                         lambda: view(0))

        def second():
            for i, sign in enumerate((1, -1)):
                k = (z + Z - sign * near) % Z
                on = k // zh == c
                for q in range(near, 0, -1):
                    lo, m, rs = (0, n, whole) if q < near else (
                        (0, cut, half_a) if sign > 0 else (cut, n - cut, half_b))

                    @pl.when(on)
                    def _():
                        if q == near:
                            landed(view(k), whole + k % zh)
                        push(view(k, lo, m), view(k, lo, m), ss2 + 2 * (q - 1) + i, rs + k % zh,
                             dev(sign * q), on, lambda lo=lo, m=m: view(0, lo, m))

        def third():
            for dz in range(1, Z):
                if dz in (near, Z - near):
                    continue
                k = (z + Z - dz) % Z

                @pl.when(k // zh == c)
                def _():
                    if dz == Z // 2:
                        landed(view(k, 0, cut), half_a + k % zh)
                        landed(view(k, cut, n - cut), half_b + k % zh)
                    else:
                        landed(view(k), whole + k % zh)

        return first, second, third

    far = sorted(range(Z), key=lambda dz: -min(dz, Z - dz))
    others = [(dz, dy) for dz in far for dy in range(YL) if dz or dy]
    half_pieces = zh * YL

    def sum_maker(it, buf, g, got, size):
        s1, r1, s2, r2 = slot(), slot(), slot(), slot()
        rows = lambda y_: pl.ds(pl.multiple_of(y_ * size, 16), size)

        def some(cnt):
            return lambda: got.at[it, pl.ds(1, cnt)]

        def first():
            for dz, dy in others:
                z_, y_ = (z + dz) % Z, (y + dy) % YL

                @pl.when(z_ // zh == c)
                def _():
                    place = (Z - dz) % Z * YL + (YL - dy) % YL
                    rcopy(g.at[it, z_ % zh, rows(y_)], got.at[it, place], s1, r1,
                          (e, row_of(z_, y_, c))).start()

            sends.append((mine, some(half_pieces - 1), s1))
            sends.append((other_core, some(half_pieces), s1))

        def second():
            @pl.when(mine)
            def _():
                landed(got.at[it, pl.ds(1, Z * YL - 1)], r1)
                val = g[it, zi, rows(y), :].astype(f32)
                for i in range(1, Z * YL):
                    val = val + got[it, i].astype(f32)
                old = buf[it, zi, rows(y), :].astype(f32)
                buf[it + 1, zi, rows(y), :] = (old - STEP_RATE * val).astype(bf16)
                piece = buf.at[it + 1, zi, rows(y)]
                for dz, dy in others:
                    rcopy(piece, piece, s2, r2,
                          (e, row_of((z + dz) % Z, (y + dy) % YL, c))).start()

            sends.append((mine, some(Z * YL - 1), s2))

        def third():
            @pl.when(mine)
            def _():
                landed(got.at[it, pl.ds(1, half_pieces - 1)], r2)

            @pl.when(other_core)
            def _():
                landed(got.at[it, pl.ds(1, half_pieces)], r2)

        return first, second, third

    def chunk_sum_maker(it):
        near = Z // 4
        n, cut, piece = s.na, s.na // 32 * 16, s.pa
        s_far, r_far, s_near, r_near = slot(2 * near), slot(2 * near), slot(2 * near), slot(2 * near)
        s1, r1, s2, r2 = slot(YL), slot(YL), slot(YL), slot(YL)
        dev = lambda dz: (e, row_of((z + Z + dz) % Z, y, c))
        rows = lambda y_: pl.ds(pl.multiple_of(y_ * piece, 16), piece)

        def part(i, q):
            return (0, n) if q < near else ((0, cut) if i == 0 else (cut, n - cut))

        def step1():
            for q in range(near, 0, -1):
                for i, sign in enumerate((1, -1)):
                    d = (z + Z + sign * (q + near)) % Z
                    on = d // zh == c
                    lo, m = part(i, q)

                    @pl.when(on)
                    def _():
                        push(ga.at[it, d % zh, pl.ds(lo, m)], rly.at[it, i, q - 1, pl.ds(lo, m)],
                             s_far + 2 * (q - 1) + i, r_far + 2 * (q - 1) + i, dev(sign * q), on,
                             lambda lo=lo, m=m: ga.at[it, 0, pl.ds(lo, m)])

            for q in range(near - 1, 0, -1):
                for i, sign in enumerate((1, -1)):
                    d = (z + Z + sign * q) % Z
                    on = d // zh == c

                    @pl.when(on)
                    def _():
                        push(ga.at[it, d % zh], gin.at[it, i, q - 1], s_near + 2 * (q - 1) + i,
                             r_near + 2 * (q - 1) + i, dev(sign * q), on, lambda: ga.at[it, 0])

        def step2():
            for i, sign in enumerate((1, -1)):
                d = (z + Z + sign * near) % Z
                on = d // zh == c

                @pl.when(on)
                def _():
                    for q in range(near, 0, -1):
                        lo, m = part(i, q)
                        landed(rly.at[it, i, q - 1, pl.ds(lo, m)], r_far + 2 * (q - 1) + i)
                    for lo, m in (part(0, near), part(1, near)):
                        val = ga[it, d % zh, lo : lo + m, :].astype(f32)
                        for q in range(1, near + 1):
                            if q < near or (lo, m) == part(i, near):
                                val = val + rly[it, i, q - 1, lo : lo + m, :].astype(f32)
                        rsum[it, i, lo : lo + m, :] = val.astype(bf16)
                    push(rsum.at[it, i], gin.at[it, i, near - 1], s_near + 2 * (near - 1) + i,
                         r_near + 2 * (near - 1) + i, dev(sign * near), on, lambda: rsum.at[it, 0])

        def first():
            @pl.when(mine)
            def _():
                val = ga[it, zi].astype(f32)
                for q in range(1, near + 1):
                    for i in range(2):
                        landed(gin.at[it, i, q - 1], r_near + 2 * (q - 1) + i)
                        val = val + gin[it, i, q - 1].astype(f32)
                val = jnp.concatenate([val, jnp.zeros((s.na_pad - n, LANES), f32)], axis=0)
                val = val.reshape(YL, piece, LANES)
                ya[...] = val
                yas[it] = val.astype(bf16)
                for dy in range(1, YL):
                    o = (y + dy) % YL
                    push(yas.at[it, o], yar.at[it, y], s1 + dy, r1 + dy, (e, row_of(z, o, c)), mine,
                         lambda: yas.at[it, 0])

        def second():
            @pl.when(mine)
            def _():
                val = ya[y]
                for dy in range(1, YL):
                    o = (y + YL - dy) % YL
                    landed(yar.at[it, o], r1 + dy)
                    val = val + yar[it, o].astype(f32)
                old = a[it, zi, rows(y), :].astype(f32)
                a[it + 1, zi, rows(y), :] = (old - STEP_RATE * val).astype(bf16)
                new = a.at[it + 1, zi, rows(y)]
                for dy in range(1, YL):
                    push(new, new, s2 + dy, r2 + dy, (e, row_of(z, (y + dy) % YL, c)), mine,
                         lambda: yas.at[it, 0])

        def third():
            @pl.when(mine)
            def _():
                for dy in range(1, YL):
                    landed(a.at[it + 1, zi, rows((y + YL - dy) % YL)], r2 + dy)

        return step1, step2, first, second, third

    def exp_maker(it, w):
        i1, s2, r2 = slot(), slot(X), slot(X)
        peer = (x * YH + 1 - yh, r)

        def first(val):
            e1s[it, w] = val.astype(bf16)
            push(e1s.at[it, w], e1r.at[it, w], i1, i1, peer)

        def second():
            landed(e1r.at[it, w], i1)
            e2s[it, w] = (e1s[it, w].astype(f32) + e1r[it, w].astype(f32)).astype(bf16)
            for dx in range(1, X):
                push(e2s.at[it, w], e2r.at[it, w, dx], s2 + dx, r2 + dx,
                     (((x + dx) % X) * YH + yh, r))

        def third():
            val = e2s[it, w].astype(f32)
            for dx in range(1, X):
                landed(e2r.at[it, w, dx], r2 + dx)
                val = val + e2r[it, w, dx].astype(f32)
            return val

        return first, second, third

    @pl.when(mine)
    def _():
        for y_ in range(YL):
            for c_ in range(2):
                @pl.when(jnp.logical_not(jnp.logical_and(y_ == y, c_ == c)))
                def _():
                    landed(bg.at[bg_rows(y_, c_)], gather_r + 2 * y_ + c_)
        for i in range(s.nt):
            tile = bg[i * LANES : (i + 1) * LANES, :].astype(f32).T
            a[0, zi, i * s.hc : (i + 1) * s.hc, :] = tile[: s.hc].astype(bf16)

    ag1, ag2, ag3 = ag_maker(a, 0, s.na_base)
    pl.when(mine)(ag1)
    ld_cal.wait()
    mask_own = rcol[...] == e.astype(f32)
    pad_rows = LANES - s.hc

    def hot(h):
        grp = lax.broadcasted_iota(jnp.int32, (t, s.el), 1) // RANK + h * (s.experts // 2)
        return jnp.concatenate([rcol[...]] * s.lb, axis=1) == grp.astype(f32)

    for it in range(ITERS):
        in_i = slot()
        upt = jnp.concatenate([b[it, k] for k in range(zh)], axis=1)
        upt = jnp.concatenate([upt, upt], axis=0)
        if it == 0:
            part = dot_t(calh[own_rows, :], upt)
            landed(calh.at[oth_rows], cal_i)
            xin_s[it] = pack(dot_t(calh[oth_rows, :], upt))
            push(xin_s.at[it], xin_r.at[it], in_i, in_i, partner)
        else:
            xin_s[it] = pack(dot_t(calh[oth_rows, :], upt))
            push(xin_s.at[it], xin_r.at[it], in_i, in_i, partner)
            part = dot_t(calh[own_rows, :], upt)
        landed(xin_r.at[it], in_i)
        inner = ((part + unpack(xin_r[it])) * inv_d).astype(bf16).astype(f32)
        inner = jnp.where(mask_own, inner, 0.0)
        x1, x2, x3 = exp_maker(it, 0)
        x1(pack(inner))
        if it == 0:
            ag2()
            d0_s, d0_r = slot(s.experts), slot(s.experts)
            for de in range(1, s.experts):
                other = (e + de) % s.experts
                push(d0s.at[other], d0r.at[e], d0_s + de, d0_r + de, (other, r))
            d0r[e] = d0s[e]
        x2()
        ag3()
        if it > 0:
            dn_i = slot()
            push(a.at[it, :, pl.ds(s.na_base, s.dr)], dnr.at[it], dn_i, dn_i, partner)
        bt = jnp.concatenate(
            [a[it, k, i * s.hc : (i + 1) * s.hc, :] for k in range(zh) for i in range(s.nt)], axis=1)
        if pad_rows:
            bt = jnp.concatenate([bt, jnp.zeros((pad_rows, s.dh), bf16)], axis=0)
        xb_i = slot()
        xb_s[it] = dot_t(calh[oth_rows, :], bt)
        push(xb_s.at[it], xb_r.at[it], xb_i, xb_i, partner)
        part = dot_t(calh[own_rows, :], bt)
        inner = unpack(x3())
        wide = jnp.concatenate([inner] * s.lb, axis=1)
        for h in range(2):
            ixs[it, h] = jnp.where(hot(h), wide, 0.0).astype(bf16)
        ix_i = slot()
        ixc[it, c] = ixs[it, c]
        push(ixs.at[it, 1 - c], ixc.at[it, c], ix_i, ix_i, partner)
        if it == 0:
            for de in range(1, s.experts):
                landed(d0r.at[(e + s.experts - de) % s.experts], d0_r + de)
            for h in range(2):
                for l in range(s.lb):
                    j = (h * s.lb + l) * 2
                    pair = d0r[j].astype(f32) + pltpu.roll(d0r[j + 1].astype(f32), RANK, 1)
                    dn[0, h, :, l * LANES : (l + 1) * LANES] = pair.astype(bf16)
            for p in range(zh):
                l, h = p // 2, p % 2
                a[0, p, s.na_base : s.na, :] = dn[
                    0, c, h * s.dr : (h + 1) * s.dr, l * LANES : (l + 1) * LANES]
        else:
            landed(dnr.at[it], dn_i)
            for p in range(zh):
                l, h = p // 2, p % 2
                at = (slice(h * s.dr, (h + 1) * s.dr), slice(l * LANES, (l + 1) * LANES))
                dn[(it, c) + at] = a[it, p, s.na_base : s.na, :]
                dn[(it, 1 - c) + at] = dnr[it, p]
        dnw = [dn[it, h] for h in range(2)]
        if pad_rows:
            dnw = [jnp.concatenate([w, jnp.zeros((pad_rows, s.el), bf16)], axis=0) for w in dnw]
        delta = dot_t(ixs[it, 0], dnw[0]) + dot_t(ixs[it, 1], dnw[1])
        delta = (delta * inv_r).astype(bf16).astype(f32)
        landed(xb_r.at[it], xb_i)
        cols = ((part + xb_r[it]) * inv_d).astype(bf16).astype(f32)
        resid = (cols + delta - tcol[...]).astype(bf16)
        res[it, c] = resid
        re_i = slot()
        push(res.at[it, c], res.at[it, c], re_i, re_i, partner)

        fold = jnp.zeros((t, LANES), f32)
        for h in range(2):
            share = jnp.where(hot(h), dot(resid, dnw[h]), 0.0)
            for l in range(s.lb):
                fold = fold + share[:, l * LANES : (l + 1) * LANES]
        fold = (fold + pltpu.roll(fold, RANK, 1)) * inv_r
        b1, b2, b3 = exp_maker(it, 1)
        b1(pack(fold))

        landed(res.at[it, 1 - c], re_i)
        rt = jnp.concatenate([res[it, 0], res[it, 1]], axis=0).astype(f32).T[: s.hc].astype(bf16)
        grad = dot(rt, calh[...]) * inv_t
        for k in range(zh):
            for i in range(s.nt):
                lo = k * s.cw + i * LANES
                ga[it, k, i * s.hc : (i + 1) * s.hc, :] = grad[:, lo : lo + LANES].astype(bf16)
        landed(ixc.at[it, 1 - c], ix_i)
        grad = dot(rt, jnp.concatenate([ixc[it, 0], ixc[it, 1]], axis=0)) * inv_t
        for p in range(zh):
            l, h = p // 2, p % 2
            ga[it, p, s.na_base : s.na, :] = grad[
                h * s.dr : (h + 1) * s.dr, l * LANES : (l + 1) * LANES].astype(bf16)
        rs1, rs2, ya1, ya2, ya3 = chunk_sum_maker(it)
        rs1()
        b2()
        rs2()
        bk = unpack(b3()).astype(bf16).astype(f32)
        back[it, c] = jnp.where(mask_own, bk, 0.0).astype(bf16)
        bk_i = slot()
        push(back.at[it, c], back.at[it, c], bk_i, bk_i, partner)
        landed(back.at[it, 1 - c], bk_i)
        bt = jnp.concatenate([back[it, 0], back[it, 1]], axis=0).astype(f32).T[:RANK].astype(bf16)
        grad = dot(bt, calh[...]) * inv_t
        for k in range(zh):
            gb[it, k] = grad[:, k * s.cw : (k + 1) * s.cw].astype(bf16)
        yb1, yb2, yb3 = sum_maker(it, b, gb, gbr, s.pb)
        yb1()
        ya1()
        ya2()
        yb2()
        ya3()
        last = it == ITERS - 1
        if not last:
            ag1, ag2, ag3 = ag_maker(a, it + 1, s.na)
            pl.when(mine)(ag1)
            ag2()
        else:
            bf_i, dn_s, dn_r = slot(), slot(Z), slot(zh)
            dn_of = lambda k: a.at[ITERS, k, pl.ds(s.na_base, s.dr)]

            @pl.when(mine)
            def _():
                for dz in far[:-1]:
                    push(dn_of(zi), dn_of(zi), dn_s + dz, dn_r + zi,
                         (e, row_of((z + dz) % Z, y, c)), mine, lambda: dn_of(0))
                push(a.at[ITERS, zi, pl.ds(0, s.na_base)], bfin, bf_i, bf_i, partner, mine,
                     lambda: bfin)
                bfin[...] = a[ITERS, zi, : s.na_base, :]

            for k in range(zh):
                @pl.when(c * zh + k != z)
                def _():
                    landed(dn_of(k), dn_r + k)
        if not last:
            yb3()

    fs, fr, fc = slot(2 * s.lb), slot(s.experts), slot()
    for l in range(s.lb):
        for h in range(YH):
            other = (s.lb * c + l) * YH + h
            away = other != e
            src = a.at[ITERS, pl.ds(2 * l, 2), pl.ds(s.na_base, s.dr)]

            @pl.when(away)
            def _():
                push(src, dnf.at[e], fs + 2 * l + h, fr + e, (other, r), away, lambda: a.at[ITERS, pl.ds(0, 2), pl.ds(s.na_base, s.dr)])

            @pl.when(other == e)
            def _():
                dnf[e] = a[ITERS, 2 * l : 2 * l + 2, s.na_base : s.na, :]

    @pl.when(other_core)
    def _():
        landed(bfin, bf_i)

    for i in range(s.nt):
        tile = bfin[i * s.hc : (i + 1) * s.hc, :].astype(f32)
        if pad_rows:
            tile = jnp.concatenate([tile, jnp.zeros((pad_rows, LANES), f32)], axis=0)
        fin[i * LANES : (i + 1) * LANES, :] = tile.T
    rows = pl.ds(pl.multiple_of((2 * y + c) * s.db, 16), s.db)
    o_base[...] = fin[rows, :][:, : s.hc].astype(bf16)

    owner = x // s.lb == c

    @pl.when(owner)
    def _():
        for j in range(s.experts):
            @pl.when(j != e)
            def _():
                landed(dnf.at[j], fr + j)
        push(dnf, dnf, fc, fc, partner, owner)

    yb3()
    fb = slot()
    push(b.at[ITERS], bo, fb, fb, partner)

    @pl.when(jnp.logical_not(owner))
    def _():
        landed(dnf, fc)

    for j in range(s.experts):
        blk = dnf[j].reshape(s.hc, LANES).astype(f32)
        blk = jnp.where(yh == 0, blk, pltpu.roll(blk, RANK, 1))
        fdn[j * s.hc : (j + 1) * s.hc, :] = blk
    o_down[...] = fdn[...].T[:RANK].astype(bf16)
    up_cols = lambda c_, k: pl.ds(pl.multiple_of(c_ * s.dh + k * s.cw, LANES), s.cw)
    for k in range(zh):
        o_up[:, up_cols(c, k)] = b[ITERS, k]
    landed(bo, fb)
    for k in range(zh):
        o_up[:, up_cols(1 - c, k)] = bo[k]

    for cond, src, ss in sends:
        src = src()
        cp = rcopy(src, src, ss, ss, partner)
        if cond is None:
            cp.wait_send()
        else:
            pl.when(cond)(cp.wait_send)


def body(calib, target, route, base, up_factor, down_factor):
    t, width = calib.shape
    s = Sizes(t, width, base.shape[1], down_factor.shape[2])
    n_sem = 320
    any_spec = pl.BlockSpec(memory_space=pl.ANY)
    vmem = pl.BlockSpec(memory_space=pltpu.VMEM)
    scratch = scratch_of(s)
    scratch["send"] = pltpu.SemaphoreType.DMA((n_sem,))
    scratch["recv"] = pltpu.SemaphoreType.DMA((n_sem,))
    hid = down_factor.shape[2]
    o_base, o_up, o_down = pl.pallas_call(
        functools.partial(kernel, s, n_sem),
        out_shape=(
            jax.ShapeDtypeStruct(base.shape, bf16),
            jax.ShapeDtypeStruct((RANK, width), bf16),
            jax.ShapeDtypeStruct((RANK, hid), bf16),
        ),
        in_specs=[any_spec] * 6,
        out_specs=(vmem, vmem, vmem),
        scratch_shapes=scratch,
        compiler_params=pltpu.CompilerParams(
            collective_id=0, has_side_effects=True, vmem_limit_bytes=56 * 1024 * 1024
        ),
        name="refine",
    )(calib, target.T, route[None], base, up_factor[0].T, down_factor[0])
    return o_base, o_up.T[None], o_down[None]


def solution(mesh):
    in_specs = (
        P("rows", None),
        P("rows", "exp"),
        P("rows"),
        P("rows", "exp"),
        P("exp", None, None),
        P("exp", None, None),
    )
    out_specs = (P("rows", "exp"), P("exp", None, None), P("exp", None, None))
    return jax.shard_map(body, mesh=mesh, in_specs=in_specs, out_specs=out_specs, check_vma=False)
```

```python
import functools
import math

import jax
import jax.numpy as jnp
from jax import lax
from jax.experimental import pallas as pl
from jax.experimental.pallas import tpu as pltpu
from jax.sharding import PartitionSpec as P

ITERS = 2
STEP_RATE = 0.25

X, YH, Z, YL = 4, 2, 8, 4
RANK = 64
LANES = 128

f32, bf16 = jnp.float32, jnp.bfloat16
MESH = pl.DeviceIdType.MESH


def dot(a, b):
    return jnp.dot(a, b, preferred_element_type=f32)


def dot_t(a, b):
    return lax.dot_general(a, b, (((1,), (1,)), ((), ())), preferred_element_type=f32)


class Sizes:
    def __init__(self, tok, width, hid, exp_hidden):
        self.t = tok
        self.dh = width // 2
        self.hc = hid
        self.zh = Z // 2
        self.cw = width // Z
        self.nt = self.cw // LANES
        self.db = width // (Z * YL * 2)
        self.experts = X * YH
        self.el = self.experts * RANK // 2
        self.lb = self.el // LANES
        self.dr = hid // 2
        self.na_base = self.nt * hid
        self.na = self.na_base + self.dr
        step = 16 * YL
        self.na_pad = -(-self.na // step) * step
        self.pa = self.na_pad // YL
        self.pb = RANK // YL
        self.tp = -(-tok // LANES) * LANES
        assert self.zh == 2 * self.lb and self.pb % 16 == 0 and self.na % 16 == 0


def scratch_of(s):
    vm = pltpu.VMEM
    return dict(
        calh=vm((2 * s.t, s.dh), bf16),
        calo=vm((s.t, s.dh), bf16),
        uph=vm((RANK, s.dh), bf16),
        tgt=vm((s.hc, s.t), bf16),
        rou=vm((1, s.t), jnp.int32),
        bas=vm((s.db, s.hc), bf16),
        dwn=vm((RANK, s.experts * s.hc), bf16),
        bpad=vm((s.db, LANES), bf16),
        bg=vm((s.cw, LANES), bf16),
        tpad=vm((LANES, s.tp), f32),
        tcol=vm((s.t, LANES), f32),
        rcol=vm((s.t, LANES), f32),
        d0s=vm((s.experts, s.hc, LANES), bf16),
        d0r=vm((s.experts, s.hc, LANES), bf16),
        a=vm((ITERS + 1, s.zh, s.na_pad, LANES), bf16),
        b=vm((ITERS + 1, s.zh, RANK, s.cw), bf16),
        bo=vm((s.zh, RANK, s.cw), bf16),
        dn=vm((ITERS, 2, s.hc, s.el), bf16),
        dnr=vm((ITERS, s.zh, s.dr, LANES), bf16),
        ga=vm((ITERS, s.zh, s.na, LANES), bf16),
        rly=vm((ITERS, 2, Z // 4, s.na, LANES), bf16),
        rsum=vm((ITERS, 2, s.na, LANES), bf16),
        gin=vm((ITERS, 2, Z // 4, s.na, LANES), bf16),
        ya=vm((YL, s.pa, LANES), f32),
        yas=vm((ITERS, YL, s.pa, LANES), bf16),
        yar=vm((ITERS, YL, s.pa, LANES), bf16),
        gb=vm((ITERS, s.zh, RANK, s.cw), bf16),
        gbr=vm((ITERS, Z * YL, s.pb, s.cw), bf16),
        xin_s=vm((ITERS, s.t // 2, LANES), f32),
        xin_r=vm((ITERS, s.t // 2, LANES), f32),
        xb_s=vm((ITERS, s.t, LANES), f32),
        xb_r=vm((ITERS, s.t, LANES), f32),
        e1s=vm((ITERS, 2, s.t // 2, LANES), bf16),
        e1r=vm((ITERS, 2, s.t // 2, LANES), bf16),
        e2s=vm((ITERS, 2, s.t // 2, LANES), bf16),
        e2r=vm((ITERS, 2, X, s.t // 2, LANES), bf16),
        ixs=vm((ITERS, 2, s.t, s.el), bf16),
        ixc=vm((ITERS, 2, s.t, s.el), bf16),
        res=vm((ITERS, 2, s.t, LANES), bf16),
        back=vm((ITERS, 2, s.t, LANES), bf16),
        bfin=vm((s.na_base, LANES), bf16),
        fin=vm((s.cw, LANES), f32),
        dnf=vm((s.experts, 2, s.dr, LANES), bf16),
        fdn=vm((s.experts * s.hc, LANES), f32),
        local_sem=pltpu.SemaphoreType.DMA((7,)),
    )


def kernel(s, n_sem, calib, target, route, base, up, down, o_base, o_up, o_down, *, send, recv,
           calh, calo, uph, tgt, rou, bas, dwn, bpad, bg, tpad, tcol, rcol, d0s, d0r, a, b, bo, dn, dnr,
           ga, rly, rsum, gin, ya, yas, yar, gb, gbr, xin_s, xin_r, xb_s, xb_r,
           e1s, e1r, e2s, e2r, ixs, ixc, res, back, bfin, fin, dnf, fdn, local_sem):
    t, zh = s.t, s.zh
    width = 2 * s.dh
    inv_d = 1.0 / math.sqrt(width)
    inv_r = 1.0 / math.sqrt(RANK)
    inv_t = 1.0 / math.sqrt(t * Z * YL * 2)

    e, r = lax.axis_index("exp"), lax.axis_index("rows")
    x, yh = e // YH, e % YH
    c, y, z = r % 2, (r // 2) % YL, r // (2 * YL)
    cz = z // zh
    zi = z % zh
    mine = cz == c
    other_core = cz != c
    row_of = lambda z_, y_, c_: (z_ * YL + y_) * 2 + c_
    partner = (e, row_of(z, y, 1 - c))

    used = [0]
    sends = []

    def slot(n=1):
        used[0] += n
        assert used[0] <= n_sem
        return used[0] - n

    def rcopy(src, dst, ss, rs, dev):
        return pltpu.make_async_remote_copy(
            src_ref=src, dst_ref=dst, send_sem=send.at[ss], recv_sem=recv.at[rs],
            device_id=dev, device_id_type=MESH)

    def push(src, dst, ss, rs, dev, cond=None, like=None):
        rcopy(src, dst, ss, rs, dev).start()
        sends.append((cond, like or (lambda: src), ss))

    def landed(dst, rs):
        rcopy(dst, dst, rs, rs, partner).wait_recv()

    lane = lax.broadcasted_iota(jnp.int32, (t // 2, LANES), 1) < RANK

    def pack(v):
        return jnp.where(lane, v[: t // 2], v[t // 2 :])

    def unpack(v):
        w = pltpu.roll(v, RANK, 1)
        return jnp.concatenate([jnp.where(lane, v, w), jnp.where(lane, w, v)], axis=0)

    own_rows = pl.ds(pl.multiple_of(c * t, t), t)
    oth_rows = pl.ds(pl.multiple_of((1 - c) * t, t), t)
    own_cols = pl.ds(pl.multiple_of(c * s.dh, LANES), s.dh)
    oth_cols = pl.ds(pl.multiple_of((1 - c) * s.dh, LANES), s.dh)
    ld_cal, ld_up, ld_tgt, ld_rou, ld_bas, ld_dwn, ld_oth = [
        pltpu.make_async_copy(src, dst, local_sem.at[i]) for i, (src, dst) in enumerate((
            (calib.at[:, own_cols], calh.at[own_rows]), (up.at[:, own_cols], uph), (target, tgt),
            (route, rou), (base, bas), (down, dwn), (calib.at[:, oth_cols], calo)))]
    for ld in (ld_bas, ld_dwn, ld_oth, ld_cal, ld_up, ld_tgt, ld_rou):
        ld.start()

    bar = pltpu.get_barrier_semaphore()
    peers = [partner]
    for dz in range(1, Z):
        peers.append((e, row_of((z + dz) % Z, y, c)))
    for dy in range(1, YL):
        for c_ in (c, 1 - c):
            peers.append((e, row_of(z, (y + dy) % YL, c_)))
    for de in range(1, s.experts):
        peers.append(((e + de) % s.experts, r))
    for dev in peers:
        pl.semaphore_signal(bar, inc=1, device_id=dev, device_id_type=MESH)
    bpad[...] = jnp.zeros_like(bpad)
    ld_bas.wait()
    bpad[:, : s.hc] = bas[...]
    ld_dwn.wait()
    dt = jnp.concatenate([dwn[...].astype(f32), jnp.zeros_like(dwn, dtype=f32)], axis=0).T
    for j in range(s.experts):
        d0s[j] = dt[j * s.hc : (j + 1) * s.hc].astype(bf16)
    pl.semaphore_wait(bar, len(peers))

    gather_s, gather_r = slot(YL), slot(2 * YL)
    bg_rows = lambda y_, c_: pl.ds(pl.multiple_of((2 * y_ + c_) * s.db, 16), s.db)
    for dy in range(1, YL):
        push(bpad, bg.at[bg_rows(y, c)], gather_s + dy, gather_r + 2 * y + c,
             (e, row_of(z, (y + dy) % YL, cz)))

    @pl.when(other_core)
    def _():
        push(bpad, bg.at[bg_rows(y, c)], gather_s, gather_r + 2 * y + c, partner, other_core)

    @pl.when(mine)
    def _():
        bg[bg_rows(y, c), :] = bpad[...]

    cal_i = slot()
    ld_oth.wait()
    push(calo, calh.at[own_rows], cal_i, cal_i, partner)

    a[0, :, s.na :, :] = jnp.zeros((zh, s.na_pad - s.na, LANES), bf16)

    ld_up.wait()
    for k in range(zh):
        b[0, k] = uph[:, k * s.cw : (k + 1) * s.cw]
    tpad[...] = jnp.zeros_like(tpad)
    ld_tgt.wait()
    tpad[: s.hc, : s.t] = tgt[...].astype(f32)
    tcol[...] = tpad[...].T[: s.t]
    ld_rou.wait()
    tpad[:, : s.t] = jnp.broadcast_to(rou[...].astype(f32), (LANES, s.t))
    rcol[...] = tpad[...].T[: s.t]

    def ag_maker(buf, v, n):
        near = Z // 4
        ss, ss2 = slot(2 * near), slot(2 * near)
        whole, half_a, half_b = slot(zh), slot(zh), slot(zh)
        cut = n // 32 * 16
        view = lambda k, lo=0, m=n: buf.at[v, k % zh, pl.ds(lo, m)]
        dev = lambda dz: (e, row_of((z + Z + dz) % Z, y, c))

        def first():
            for q in range(near, 0, -1):
                for i, sign in enumerate((1, -1)):
                    push(view(z), view(z), ss + 2 * (q - 1) + i, whole + zi, dev(sign * q), mine,
                         lambda: view(0))

        def second():
            for i, sign in enumerate((1, -1)):
                k = (z + Z - sign * near) % Z
                on = k // zh == c
                for q in range(near, 0, -1):
                    lo, m, rs = (0, n, whole) if q < near else (
                        (0, cut, half_a) if sign > 0 else (cut, n - cut, half_b))

                    @pl.when(on)
                    def _():
                        if q == near:
                            landed(view(k), whole + k % zh)
                        push(view(k, lo, m), view(k, lo, m), ss2 + 2 * (q - 1) + i, rs + k % zh,
                             dev(sign * q), on, lambda lo=lo, m=m: view(0, lo, m))

        def third():
            for dz in range(1, Z):
                if dz in (near, Z - near):
                    continue
                k = (z + Z - dz) % Z

                @pl.when(k // zh == c)
                def _():
                    if dz == Z // 2:
                        landed(view(k, 0, cut), half_a + k % zh)
                        landed(view(k, cut, n - cut), half_b + k % zh)
                    else:
                        landed(view(k), whole + k % zh)

        return first, second, third

    far = sorted(range(Z), key=lambda dz: -min(dz, Z - dz))
    others = [(dz, dy) for dz in far for dy in range(YL) if dz or dy]
    half_pieces = zh * YL

    def sum_maker(it, buf, g, got, size):
        s1, r1, s2, r2 = slot(), slot(), slot(), slot()
        rows = lambda y_: pl.ds(pl.multiple_of(y_ * size, 16), size)

        def some(cnt):
            return lambda: got.at[it, pl.ds(1, cnt)]

        def first():
            for dz, dy in others:
                z_, y_ = (z + dz) % Z, (y + dy) % YL

                @pl.when(z_ // zh == c)
                def _():
                    place = (Z - dz) % Z * YL + (YL - dy) % YL
                    rcopy(g.at[it, z_ % zh, rows(y_)], got.at[it, place], s1, r1,
                          (e, row_of(z_, y_, c))).start()

            sends.append((mine, some(half_pieces - 1), s1))
            sends.append((other_core, some(half_pieces), s1))

        def second():
            @pl.when(mine)
            def _():
                landed(got.at[it, pl.ds(1, Z * YL - 1)], r1)
                val = g[it, zi, rows(y), :].astype(f32)
                for i in range(1, Z * YL):
                    val = val + got[it, i].astype(f32)
                old = buf[it, zi, rows(y), :].astype(f32)
                buf[it + 1, zi, rows(y), :] = (old - STEP_RATE * val).astype(bf16)
                piece = buf.at[it + 1, zi, rows(y)]
                for dz, dy in others:
                    rcopy(piece, piece, s2, r2,
                          (e, row_of((z + dz) % Z, (y + dy) % YL, c))).start()

            sends.append((mine, some(Z * YL - 1), s2))

        def third():
            @pl.when(mine)
            def _():
                landed(got.at[it, pl.ds(1, half_pieces - 1)], r2)

            @pl.when(other_core)
            def _():
                landed(got.at[it, pl.ds(1, half_pieces)], r2)

        return first, second, third

    def chunk_sum_maker(it):
        near = Z // 4
        n, cut, piece = s.na, s.na // 32 * 16, s.pa
        s_far, r_far, s_near, r_near = slot(2 * near), slot(2 * near), slot(2 * near), slot(2 * near)
        s1, r1, s2, r2 = slot(YL), slot(YL), slot(YL), slot(YL)
        dev = lambda dz: (e, row_of((z + Z + dz) % Z, y, c))
        rows = lambda y_: pl.ds(pl.multiple_of(y_ * piece, 16), piece)

        def part(i, q):
            return (0, n) if q < near else ((0, cut) if i == 0 else (cut, n - cut))

        def step1():
            for q in range(near, 0, -1):
                for i, sign in enumerate((1, -1)):
                    d = (z + Z + sign * (q + near)) % Z
                    on = d // zh == c
                    lo, m = part(i, q)

                    @pl.when(on)
                    def _():
                        push(ga.at[it, d % zh, pl.ds(lo, m)], rly.at[it, i, q - 1, pl.ds(lo, m)],
                             s_far + 2 * (q - 1) + i, r_far + 2 * (q - 1) + i, dev(sign * q), on,
                             lambda lo=lo, m=m: ga.at[it, 0, pl.ds(lo, m)])

            for q in range(near - 1, 0, -1):
                for i, sign in enumerate((1, -1)):
                    d = (z + Z + sign * q) % Z
                    on = d // zh == c

                    @pl.when(on)
                    def _():
                        push(ga.at[it, d % zh], gin.at[it, i, q - 1], s_near + 2 * (q - 1) + i,
                             r_near + 2 * (q - 1) + i, dev(sign * q), on, lambda: ga.at[it, 0])

        def step2():
            for i, sign in enumerate((1, -1)):
                d = (z + Z + sign * near) % Z
                on = d // zh == c

                @pl.when(on)
                def _():
                    for q in range(near, 0, -1):
                        lo, m = part(i, q)
                        landed(rly.at[it, i, q - 1, pl.ds(lo, m)], r_far + 2 * (q - 1) + i)
                    for lo, m in (part(0, near), part(1, near)):
                        val = ga[it, d % zh, lo : lo + m, :].astype(f32)
                        for q in range(1, near + 1):
                            if q < near or (lo, m) == part(i, near):
                                val = val + rly[it, i, q - 1, lo : lo + m, :].astype(f32)
                        rsum[it, i, lo : lo + m, :] = val.astype(bf16)
                    push(rsum.at[it, i], gin.at[it, i, near - 1], s_near + 2 * (near - 1) + i,
                         r_near + 2 * (near - 1) + i, dev(sign * near), on, lambda: rsum.at[it, 0])

        def first():
            @pl.when(mine)
            def _():
                val = ga[it, zi].astype(f32)
                for q in range(1, near + 1):
                    for i in range(2):
                        landed(gin.at[it, i, q - 1], r_near + 2 * (q - 1) + i)
                        val = val + gin[it, i, q - 1].astype(f32)
                val = jnp.concatenate([val, jnp.zeros((s.na_pad - n, LANES), f32)], axis=0)
                val = val.reshape(YL, piece, LANES)
                ya[...] = val
                yas[it] = val.astype(bf16)
                for dy in range(1, YL):
                    o = (y + dy) % YL
                    push(yas.at[it, o], yar.at[it, y], s1 + dy, r1 + dy, (e, row_of(z, o, c)), mine,
                         lambda: yas.at[it, 0])

        def second():
            @pl.when(mine)
            def _():
                val = ya[y]
                for dy in range(1, YL):
                    o = (y + YL - dy) % YL
                    landed(yar.at[it, o], r1 + dy)
                    val = val + yar[it, o].astype(f32)
                old = a[it, zi, rows(y), :].astype(f32)
                a[it + 1, zi, rows(y), :] = (old - STEP_RATE * val).astype(bf16)
                new = a.at[it + 1, zi, rows(y)]
                for dy in range(1, YL):
                    push(new, new, s2 + dy, r2 + dy, (e, row_of(z, (y + dy) % YL, c)), mine,
                         lambda: yas.at[it, 0])

        def third():
            @pl.when(mine)
            def _():
                for dy in range(1, YL):
                    landed(a.at[it + 1, zi, rows((y + YL - dy) % YL)], r2 + dy)

        return step1, step2, first, second, third

    def exp_maker(it, w):
        i1, s2, r2 = slot(), slot(X), slot(X)
        peer = (x * YH + 1 - yh, r)

        def first(val):
            e1s[it, w] = val.astype(bf16)
            push(e1s.at[it, w], e1r.at[it, w], i1, i1, peer)

        def second():
            landed(e1r.at[it, w], i1)
            e2s[it, w] = (e1s[it, w].astype(f32) + e1r[it, w].astype(f32)).astype(bf16)
            for dx in range(1, X):
                push(e2s.at[it, w], e2r.at[it, w, dx], s2 + dx, r2 + dx,
                     (((x + dx) % X) * YH + yh, r))

        def third():
            val = e2s[it, w].astype(f32)
            for dx in range(1, X):
                landed(e2r.at[it, w, dx], r2 + dx)
                val = val + e2r[it, w, dx].astype(f32)
            return val

        return first, second, third

    @pl.when(mine)
    def _():
        for y_ in range(YL):
            for c_ in range(2):
                @pl.when(jnp.logical_not(jnp.logical_and(y_ == y, c_ == c)))
                def _():
                    landed(bg.at[bg_rows(y_, c_)], gather_r + 2 * y_ + c_)
        for i in range(s.nt):
            tile = bg[i * LANES : (i + 1) * LANES, :].astype(f32).T
            a[0, zi, i * s.hc : (i + 1) * s.hc, :] = tile[: s.hc].astype(bf16)

    ag1, ag2, ag3 = ag_maker(a, 0, s.na_base)
    pl.when(mine)(ag1)
    ld_cal.wait()
    mask_own = rcol[...] == e.astype(f32)
    pad_rows = LANES - s.hc

    def hot(h):
        grp = lax.broadcasted_iota(jnp.int32, (t, s.el), 1) // RANK + h * (s.experts // 2)
        return jnp.concatenate([rcol[...]] * s.lb, axis=1) == grp.astype(f32)

    for it in range(ITERS):
        in_i = slot()
        upt = jnp.concatenate([b[it, k] for k in range(zh)], axis=1)
        upt = jnp.concatenate([upt, upt], axis=0)
        if it == 0:
            part = dot_t(calh[own_rows, :], upt)
            landed(calh.at[oth_rows], cal_i)
            xin_s[it] = pack(dot_t(calh[oth_rows, :], upt))
            push(xin_s.at[it], xin_r.at[it], in_i, in_i, partner)
        else:
            xin_s[it] = pack(dot_t(calh[oth_rows, :], upt))
            push(xin_s.at[it], xin_r.at[it], in_i, in_i, partner)
            part = dot_t(calh[own_rows, :], upt)
        landed(xin_r.at[it], in_i)
        inner = ((part + unpack(xin_r[it])) * inv_d).astype(bf16).astype(f32)
        inner = jnp.where(mask_own, inner, 0.0)
        x1, x2, x3 = exp_maker(it, 0)
        x1(pack(inner))
        if it == 0:
            ag2()
            d0_s, d0_r = slot(s.experts), slot(s.experts)
            for de in range(1, s.experts):
                other = (e + de) % s.experts
                push(d0s.at[other], d0r.at[e], d0_s + de, d0_r + de, (other, r))
            d0r[e] = d0s[e]
        x2()
        ag3()
        if it > 0:
            dn_i = slot()
            push(a.at[it, :, pl.ds(s.na_base, s.dr)], dnr.at[it], dn_i, dn_i, partner)
        bt = jnp.concatenate(
            [a[it, k, i * s.hc : (i + 1) * s.hc, :] for k in range(zh) for i in range(s.nt)], axis=1)
        if pad_rows:
            bt = jnp.concatenate([bt, jnp.zeros((pad_rows, s.dh), bf16)], axis=0)
        xb_i = slot()
        xb_s[it] = dot_t(calh[oth_rows, :], bt)
        push(xb_s.at[it], xb_r.at[it], xb_i, xb_i, partner)
        part = dot_t(calh[own_rows, :], bt)
        inner = unpack(x3())
        wide = jnp.concatenate([inner] * s.lb, axis=1)
        for h in range(2):
            ixs[it, h] = jnp.where(hot(h), wide, 0.0).astype(bf16)
        ix_i = slot()
        ixc[it, c] = ixs[it, c]
        push(ixs.at[it, 1 - c], ixc.at[it, c], ix_i, ix_i, partner)
        if it == 0:
            for de in range(1, s.experts):
                landed(d0r.at[(e + s.experts - de) % s.experts], d0_r + de)
            for h in range(2):
                for l in range(s.lb):
                    j = (h * s.lb + l) * 2
                    pair = d0r[j].astype(f32) + pltpu.roll(d0r[j + 1].astype(f32), RANK, 1)
                    dn[0, h, :, l * LANES : (l + 1) * LANES] = pair.astype(bf16)
            for p in range(zh):
                l, h = p // 2, p % 2
                a[0, p, s.na_base : s.na, :] = dn[
                    0, c, h * s.dr : (h + 1) * s.dr, l * LANES : (l + 1) * LANES]
        else:
            landed(dnr.at[it], dn_i)
            for p in range(zh):
                l, h = p // 2, p % 2
                at = (slice(h * s.dr, (h + 1) * s.dr), slice(l * LANES, (l + 1) * LANES))
                dn[(it, c) + at] = a[it, p, s.na_base : s.na, :]
                dn[(it, 1 - c) + at] = dnr[it, p]
        dnw = [dn[it, h] for h in range(2)]
        if pad_rows:
            dnw = [jnp.concatenate([w, jnp.zeros((pad_rows, s.el), bf16)], axis=0) for w in dnw]
        delta = dot_t(ixs[it, 0], dnw[0]) + dot_t(ixs[it, 1], dnw[1])
        delta = (delta * inv_r).astype(bf16).astype(f32)
        landed(xb_r.at[it], xb_i)
        cols = ((part + xb_r[it]) * inv_d).astype(bf16).astype(f32)
        resid = (cols + delta - tcol[...]).astype(bf16)
        res[it, c] = resid
        re_i = slot()
        push(res.at[it, c], res.at[it, c], re_i, re_i, partner)

        fold = jnp.zeros((t, LANES), f32)
        for h in range(2):
            share = jnp.where(hot(h), dot(resid, dnw[h]), 0.0)
            for l in range(s.lb):
                fold = fold + share[:, l * LANES : (l + 1) * LANES]
        fold = (fold + pltpu.roll(fold, RANK, 1)) * inv_r
        b1, b2, b3 = exp_maker(it, 1)
        b1(pack(fold))

        landed(res.at[it, 1 - c], re_i)
        rt = jnp.concatenate([res[it, 0], res[it, 1]], axis=0).astype(f32).T[: s.hc].astype(bf16)
        grad = dot(rt, calh[...]) * inv_t
        for k in range(zh):
            for i in range(s.nt):
                lo = k * s.cw + i * LANES
                ga[it, k, i * s.hc : (i + 1) * s.hc, :] = grad[:, lo : lo + LANES].astype(bf16)
        landed(ixc.at[it, 1 - c], ix_i)
        grad = dot(rt, jnp.concatenate([ixc[it, 0], ixc[it, 1]], axis=0)) * inv_t
        for p in range(zh):
            l, h = p // 2, p % 2
            ga[it, p, s.na_base : s.na, :] = grad[
                h * s.dr : (h + 1) * s.dr, l * LANES : (l + 1) * LANES].astype(bf16)
        rs1, rs2, ya1, ya2, ya3 = chunk_sum_maker(it)
        rs1()
        b2()
        rs2()
        bk = unpack(b3()).astype(bf16).astype(f32)
        back[it, c] = jnp.where(mask_own, bk, 0.0).astype(bf16)
        bk_i = slot()
        push(back.at[it, c], back.at[it, c], bk_i, bk_i, partner)
        landed(back.at[it, 1 - c], bk_i)
        bt = jnp.concatenate([back[it, 0], back[it, 1]], axis=0).astype(f32).T[:RANK].astype(bf16)
        grad = dot(bt, calh[...]) * inv_t
        for k in range(zh):
            gb[it, k] = grad[:, k * s.cw : (k + 1) * s.cw].astype(bf16)
        yb1, yb2, yb3 = sum_maker(it, b, gb, gbr, s.pb)
        yb1()
        ya1()
        ya2()
        yb2()
        ya3()
        last = it == ITERS - 1
        if not last:
            ag1, ag2, ag3 = ag_maker(a, it + 1, s.na)
            pl.when(mine)(ag1)
            ag2()
        else:
            bf_i, dn_s, dn_r = slot(), slot(Z), slot(zh)
            dn_of = lambda k: a.at[ITERS, k, pl.ds(s.na_base, s.dr)]

            @pl.when(mine)
            def _():
                for dz in far[:-1]:
                    push(dn_of(zi), dn_of(zi), dn_s + dz, dn_r + zi,
                         (e, row_of((z + dz) % Z, y, c)), mine, lambda: dn_of(0))
                push(a.at[ITERS, zi, pl.ds(0, s.na_base)], bfin, bf_i, bf_i, partner, mine,
                     lambda: bfin)
                bfin[...] = a[ITERS, zi, : s.na_base, :]

            for k in range(zh):
                @pl.when(c * zh + k != z)
                def _():
                    landed(dn_of(k), dn_r + k)
        if not last:
            yb3()

    fs, fr, fc = slot(2 * s.lb), slot(s.experts), slot()
    for l in range(s.lb):
        for h in range(YH):
            other = (s.lb * c + l) * YH + h
            away = other != e
            src = a.at[ITERS, pl.ds(2 * l, 2), pl.ds(s.na_base, s.dr)]

            @pl.when(away)
            def _():
                push(src, dnf.at[e], fs + 2 * l + h, fr + e, (other, r), away, lambda: a.at[ITERS, pl.ds(0, 2), pl.ds(s.na_base, s.dr)])

            @pl.when(other == e)
            def _():
                dnf[e] = a[ITERS, 2 * l : 2 * l + 2, s.na_base : s.na, :]

    @pl.when(other_core)
    def _():
        landed(bfin, bf_i)

    for i in range(s.nt):
        tile = bfin[i * s.hc : (i + 1) * s.hc, :].astype(f32)
        if pad_rows:
            tile = jnp.concatenate([tile, jnp.zeros((pad_rows, LANES), f32)], axis=0)
        fin[i * LANES : (i + 1) * LANES, :] = tile.T
    rows = pl.ds(pl.multiple_of((2 * y + c) * s.db, 16), s.db)
    o_base[...] = fin[rows, :][:, : s.hc].astype(bf16)

    yb3()
    fb = slot()
    push(b.at[ITERS], bo, fb, fb, partner)

    owner = x // s.lb == c

    @pl.when(owner)
    def _():
        for j in range(s.experts):
            @pl.when(j != e)
            def _():
                landed(dnf.at[j], fr + j)
        push(dnf, dnf, fc, fc, partner, owner)

    @pl.when(jnp.logical_not(owner))
    def _():
        landed(dnf, fc)

    for j in range(s.experts):
        blk = dnf[j].reshape(s.hc, LANES).astype(f32)
        blk = jnp.where(yh == 0, blk, pltpu.roll(blk, RANK, 1))
        fdn[j * s.hc : (j + 1) * s.hc, :] = blk
    o_down[...] = fdn[...].T[:RANK].astype(bf16)
    up_cols = lambda c_, k: pl.ds(pl.multiple_of(c_ * s.dh + k * s.cw, LANES), s.cw)
    for k in range(zh):
        o_up[:, up_cols(c, k)] = b[ITERS, k]
    landed(bo, fb)
    for k in range(zh):
        o_up[:, up_cols(1 - c, k)] = bo[k]

    for cond, src, ss in sends:
        src = src()
        cp = rcopy(src, src, ss, ss, partner)
        if cond is None:
            cp.wait_send()
        else:
            pl.when(cond)(cp.wait_send)


def body(calib, target, route, base, up_factor, down_factor):
    t, width = calib.shape
    s = Sizes(t, width, base.shape[1], down_factor.shape[2])
    n_sem = 320
    any_spec = pl.BlockSpec(memory_space=pl.ANY)
    vmem = pl.BlockSpec(memory_space=pltpu.VMEM)
    scratch = scratch_of(s)
    scratch["send"] = pltpu.SemaphoreType.DMA((n_sem,))
    scratch["recv"] = pltpu.SemaphoreType.DMA((n_sem,))
    hid = down_factor.shape[2]
    o_base, o_up, o_down = pl.pallas_call(
        functools.partial(kernel, s, n_sem),
        out_shape=(
            jax.ShapeDtypeStruct(base.shape, bf16),
            jax.ShapeDtypeStruct((RANK, width), bf16),
            jax.ShapeDtypeStruct((RANK, hid), bf16),
        ),
        in_specs=[any_spec] * 6,
        out_specs=(vmem, vmem, vmem),
        scratch_shapes=scratch,
        compiler_params=pltpu.CompilerParams(
            collective_id=0, has_side_effects=True, vmem_limit_bytes=56 * 1024 * 1024
        ),
        name="refine",
    )(calib, target.T, route[None], base, up_factor[0].T, down_factor[0])
    return o_base, o_up.T[None], o_down[None]


def solution(mesh):
    in_specs = (
        P("rows", None),
        P("rows", "exp"),
        P("rows"),
        P("rows", "exp"),
        P("exp", None, None),
        P("exp", None, None),
    )
    out_specs = (P("rows", "exp"), P("exp", None, None), P("exp", None, None))
    return jax.shard_map(body, mesh=mesh, in_specs=in_specs, out_specs=out_specs, check_vma=False)
```
